32 devices in a mesh: seq: 4 (over z), ctx: 8 (over y, x, core).
Axes of the slice: x: 2, y: 2, z: 4, core: 2. Of those that a mesh axis runs over, the one named last changes fastest.
Arguments:
- tokens: bfloat16 [6144, 2048], P(('seq', 'ctx')), may hold values from -6 to 6
- segments: int32 [4, 1536], P('seq', 'ctx'), may hold values from 0 to 7, as said below
- cotangent: bfloat16 [6144, 2048], P(('seq', 'ctx')), may hold values from -6 to 6
- attention_gain: bfloat16 [2048], P(('seq', 'ctx')), may hold values from 0.5 to 1.5
- query_weight: bfloat16 [2048, 2048], P(('seq', 'ctx')), may hold values from -0.1875 to 0.1875
- key_weight: bfloat16 [2048, 256], P(('seq', 'ctx')), may hold values from -0.1875 to 0.1875
- value_weight: bfloat16 [2048, 256], P(('seq', 'ctx')), may hold values from -0.125 to 0.125
- projection: bfloat16 [2048, 2048], P(('seq', 'ctx')), may hold values from -0.5 to 0.5
- feedforward_gain: bfloat16 [2048], P(('seq', 'ctx')), may hold values from 0.5 to 1.5
- gate_weight: bfloat16 [2048, 5632], P(('seq', 'ctx')), may hold values from -0.125 to 0.125
- up_weight: bfloat16 [2048, 5632], P(('seq', 'ctx')), may hold values from -0.125 to 0.125
- down_weight: bfloat16 [5632, 2048], P(('seq', 'ctx')), may hold values from -0.078125 to 0.078125
Outputs:
- block_out: bfloat16 [6144, 2048], P(('seq', 'ctx'))
- grad_tokens: float32 [6144, 2048], P(('seq', 'ctx'))
- grad_attention: float32 [2048], P(('seq', 'ctx'))
- grad_query: float32 [2048, 2048], P(('seq', 'ctx'))
- grad_key: float32 [2048, 256], P(('seq', 'ctx'))
- grad_value: float32 [2048, 256], P(('seq', 'ctx'))
- grad_projection: float32 [2048, 2048], P(('seq', 'ctx'))
- grad_feedforward: float32 [2048], P(('seq', 'ctx'))
- grad_gate: float32 [2048, 5632], P(('seq', 'ctx'))
- grad_up: float32 [2048, 5632], P(('seq', 'ctx'))
- grad_down: float32 [5632, 2048], P(('seq', 'ctx'))
The draws below stay inside these ranges and needn't reach their ends.
Inputs may be any that keep to these rules, and one draw needn't show every extreme that they name: `segments`: segment numbers count documents from 0 along each sequence. One sequence, chosen by the seed, is a single document. Another, also chosen by the seed, is packed with documents of exactly 200 tokens. In the others the documents have 200 to 2000 tokens. In every sequence the last document may be shorter.
All inputs are finite; a program needn't handle non-finite values.
Results may differ from the reference program's by a relative error of at most 0.017.
Values may be sent and summed in bfloat16 or wider, within the bound.
No kernel may reach another device: no remote copies, remote signals or barrier semaphores. Data moves between devices by JAX's collectives and lax.ppermute only.
A program may use at most 384 MiB of HBM per device.

```python
import jax
import jax.numpy as jnp
from jax import lax

D = 2048
H = 32
KV = 4
HD = 64
FF = 5632
DOC_MIN = 200
DOC_MAX = 2000
SEQS = 4
LENGTH = 1536
TOKENS = 6144


def draw_segments(key, part):
    key = jax.random.fold_in(key, 11)
    length_key, pick_key, dense_key = jax.random.split(key, 3)
    doc_count = LENGTH // DOC_MIN + 1
    doc_lengths = jax.random.randint(length_key, (SEQS, doc_count), DOC_MIN, DOC_MAX + 1)
    single = jax.random.randint(pick_key, (), 0, SEQS)
    dense_row = (single + 1 + jax.random.randint(dense_key, (), 0, SEQS - 1)) % SEQS
    rows = jnp.arange(SEQS, dtype=jnp.int32)
    doc_lengths = jnp.where((rows == dense_row)[:, None], DOC_MIN, doc_lengths).astype(jnp.int32)
    doc_ends = jnp.cumsum(doc_lengths, axis=1).astype(jnp.int32)
    place = jnp.arange(LENGTH, dtype=jnp.int32)
    numbers = jnp.sum((doc_ends[:, None, :] <= place[None, :, None]).astype(jnp.int32), axis=2)
    packed = (rows != single)[:, None]
    return jnp.where(packed, numbers, 0).astype(jnp.int32)


def block_scale(own_key, shape, cuts, smallest, largest):
    level = 1.0
    for axis_at, blocks in cuts:
        steps = jax.random.uniform(jax.random.fold_in(jax.random.fold_in(own_key, 6), axis_at), (blocks,), jnp.float32, smallest / len(cuts), largest / len(cuts))
        level = level * jnp.repeat(jnp.exp(steps), shape[axis_at] // blocks).reshape((-1,) + (1,) * (len(shape) - 1 - axis_at))
    return level


def scatter_about(own_key, shape, spread, bound, cuts=(), held_as=jnp.bfloat16):
    factor_of = block_scale(own_key, shape, cuts, -0.22, 0.18) if cuts else 1.0
    values = jax.random.normal(own_key, shape, jnp.float32) * spread * factor_of
    return jnp.minimum(jnp.maximum(values, -bound), bound).astype(held_as)


def setup_inputs(seed: int = 0) -> dict:
    arg_keys = jax.random.split(jax.random.key(seed), 13)
    return {
        "tokens": scatter_about(arg_keys[0], (TOKENS, D), 1.0, 6.0, ((0, 32),)),
        "segments": draw_segments(jax.random.fold_in(arg_keys[12], 71), 0),
        "cotangent": scatter_about(arg_keys[2], (TOKENS, D), 1.0, 6.0, ((0, 32),)),
        "attention_gain": jnp.clip(1.0 + 0.1 * jax.random.normal(arg_keys[3], (D,), jnp.float32), 0.5, 1.5).astype(jnp.bfloat16),
        "query_weight": scatter_about(arg_keys[4], (D, D), (D // 2) ** -0.5, 0.1875, ((0, 32),)),
        "key_weight": scatter_about(arg_keys[5], (D, KV * HD), (D // 2) ** -0.5, 0.1875, ((0, 32),)),
        "value_weight": scatter_about(arg_keys[6], (D, KV * HD), D ** -0.5, 0.125, ((0, 32),)),
        "projection": scatter_about(arg_keys[7], (D, D), (D // 16) ** -0.5, 0.5, ((0, 32),)),
        "feedforward_gain": jnp.clip(1.0 + 0.1 * jax.random.normal(arg_keys[8], (D,), jnp.float32), 0.5, 1.5).astype(jnp.bfloat16),
        "gate_weight": scatter_about(arg_keys[9], (D, FF), D ** -0.5, 0.125, ((0, 32),)),
        "up_weight": scatter_about(arg_keys[10], (D, FF), D ** -0.5, 0.125, ((0, 32),)),
        "down_weight": scatter_about(arg_keys[11], (FF, D), FF ** -0.5, 0.078125, ((0, 32),)),
    }


HIGHEST = lax.Precision.HIGHEST
MASKED = -1e+30

@jax.custom_vjp
def low(v):
    return lax.optimization_barrier(v.astype(jnp.bfloat16)).astype(jnp.float32)

@jax.custom_vjp
def low_back(v):
    return v

def low_keep(v):
    return (low(v), None)

def low_pass(kept, grad):
    return (grad,)

def back_keep(v):
    return (v, None)

def back_low(kept, grad):
    return (low(grad),)
low.defvjp(low_keep, low_pass)
low_back.defvjp(back_keep, back_low)

def normalize(values, scaling):
    factor = lax.rsqrt(lax.optimization_barrier(jnp.mean(values * values, axis=-1, keepdims=True)) + 1e-05)
    return values * factor * scaling

def dense(left, right):
    return jnp.dot(left, right, precision=HIGHEST)

def rotate(source, cosine, sine_part):
    first_half = source[..., :HD // 2]
    second_half = source[..., HD // 2:]
    cos_part = cosine[:, None, :]
    sin_part = sine_part[:, None, :]
    return jnp.concatenate([first_half * cos_part - second_half * sin_part, second_half * cos_part + first_half * sin_part], axis=-1)

def attend(pieces):
    query, keyed, valued, seg_row = pieces
    length = query.shape[0]
    block = 512 if length % 512 == 0 else length
    place = jnp.arange(length, dtype=jnp.int32)
    scale = HD ** (-0.5)

    def one_block(inner):
        row_query, row_place, row_seg = inner
        grouped = row_query.reshape(block, KV, H // KV, HD)
        scores = jnp.einsum('bgie,kge->gibk', grouped, keyed, precision=HIGHEST) * scale
        allowed = (seg_row[None, :] == row_seg[:, None]) & (place[None, :] <= row_place[:, None])
        scores = low_back(jnp.where(allowed[None, None], scores, MASKED))
        top = lax.optimization_barrier(jnp.max(scores, axis=-1, keepdims=True))
        weights = jnp.exp(scores - top)
        weights = weights / lax.optimization_barrier(jnp.sum(weights, axis=-1, keepdims=True))
        mixed = jnp.einsum('gibk,kge->bgie', low(weights), valued, precision=HIGHEST)
        return mixed.reshape(block, H * HD)
    inner = (query.reshape(length // block, block, H, HD), place.reshape(length // block, block), seg_row.reshape(length // block, block))
    return lax.map(jax.checkpoint(one_block), inner).reshape(length, H * HD)

def reference(tokens, segments, cotangent, attention_gain, query_weight, key_weight, value_weight, projection, feedforward_gain, gate_weight, up_weight, down_weight):
    place = jnp.arange(LENGTH, dtype=jnp.int32)
    starts = jnp.concatenate([jnp.ones((SEQS, 1), dtype=jnp.bool_), segments[:, 1:] != segments[:, :-1]], axis=1)
    positions = place[None, :] - lax.cummax(jnp.where(starts, place[None, :], 0), axis=1)
    freqs = jnp.power(10000.0, -jnp.arange(HD // 2, dtype=jnp.float32) * (2.0 / HD))
    angles = positions.reshape(TOKENS).astype(jnp.float32)[:, None] * freqs[None, :]
    cosine = jnp.cos(angles)
    sine_part = jnp.sin(angles)

    def forward(inputs, gain_one, wide_query, wide_key, wide_value, wide_projection, gain_two, wide_gate, wide_up, wide_down):
        normed = low(normalize(inputs, gain_one))
        query = low_back(dense(normed, wide_query)).reshape(TOKENS, H, HD)
        keyed = low_back(dense(normed, wide_key)).reshape(TOKENS, KV, HD)
        valued = low(low_back(dense(normed, wide_value))).reshape(SEQS, LENGTH, KV, HD)
        query = low(rotate(query, cosine, sine_part)).reshape(SEQS, LENGTH, H, HD)
        keyed = low(rotate(keyed, cosine, sine_part)).reshape(SEQS, LENGTH, KV, HD)
        mixed = lax.map(attend, (query, keyed, valued, segments)).reshape(TOKENS, H * HD)
        attended = low(low_back(mixed))
        hidden = inputs + low_back(dense(attended, wide_projection))
        normed_two = low(normalize(hidden, gain_two))
        gate = low_back(dense(normed_two, wide_gate))
        upward = low_back(dense(normed_two, wide_up))
        activated = low(jax.nn.silu(gate) * upward)
        return hidden + low_back(dense(activated, wide_down))
    floats = [array.astype(jnp.float32) for array in (tokens, attention_gain, query_weight, key_weight, value_weight, projection, feedforward_gain, gate_weight, up_weight, down_weight)]
    outcome, pullback = jax.vjp(forward, *floats)
    grads = pullback(cotangent.astype(jnp.float32))
    return (outcome.astype(jnp.bfloat16), grads[0], grads[1], grads[2], grads[3], grads[4], grads[5], grads[6], grads[7], grads[8], grads[9])
```

```python
import functools

import jax
import jax.numpy as jnp
from jax import lax
from jax.experimental import pallas as pl
from jax.experimental.pallas import tpu as pltpu
from jax.sharding import PartitionSpec as P

H = 32
KV = 4
HD = 64
HALF = HD // 2

EPSILON = 1e-05
MASKED = -1e30
BOTH = ("seq", "ctx")
f32 = jnp.float32
bf16 = jnp.bfloat16


def dot(left, right, contract, out=f32):
    return lax.dot_general(left, right, (contract, ((), ())), preferred_element_type=f32).astype(out)


def after(value, *others):
    return lax.optimization_barrier((value, *others))[0]


def swap(value, step, count):
    return lax.ppermute(value, "ctx", [(i, i ^ step) for i in range(count)])


def blank(shape, dtype):
    return pl.pallas_call(
        lambda out_ref: None,
        out_shape=jax.ShapeDtypeStruct(shape, dtype),
        out_specs=pl.BlockSpec(memory_space=pl.ANY),
        name="blank",
    )()


def chip_bits():
    me = lax.axis_index("ctx")
    count = lax.axis_size("ctx")
    bits = [1 << at for at in range(1, count.bit_length() - 1)]
    return [(step, (me // step) % 2) for step in bits]


def gather_ctx(value):
    count = lax.axis_size("ctx")
    core = lax.axis_index("ctx") % 2
    bits = chip_bits()
    half, depth = value.shape[0] // 2, value.shape[1]
    shape = (2,) * len(bits) + (2, 2, half, depth)
    whole = blank(shape, value.dtype)

    def put(whole, part, at):
        place = [0] * len(shape)
        for axis, index in at:
            place[axis] = index
        return lax.dynamic_update_slice(whole, part, place)

    for which in range(2):
        current = value[which * half : (which + 1) * half].reshape((1,) * len(bits) + (half, depth))
        order = range(len(bits)) if which == 0 else range(len(bits) - 1, -1, -1)
        for at in order:
            step, bit = bits[at]
            axis = len(bits) - 1 - at
            arrived = swap(current, step, count)
            if at == order[-1]:
                break
            current = jnp.where(
                bit == 0,
                jnp.concatenate([current, arrived], axis),
                jnp.concatenate([arrived, current], axis),
            )
        for part, index in ((current, bit), (arrived, 1 - bit)):
            for there in range(2):
                piece = swap(part, 1, count) if there else part
                owner = 1 - core if there else core
                spots = ((axis, index), (len(bits), owner), (len(bits) + 1, which))
                piece = piece.reshape(piece.shape[:-2] + (1, 1, half, depth))
                whole = put(whole, piece, spots)
    return whole.reshape(count * value.shape[0], depth)


def of_core(value, core):
    count = lax.axis_size("ctx")
    blocks = value.reshape(count // 2, 2, value.shape[0] // count, value.shape[1])
    return lax.dynamic_index_in_dim(blocks, core, 1, keepdims=False).reshape(-1, value.shape[1])


def pair_up(left, right, contract, wait=()):
    count = lax.axis_size("ctx")
    core = lax.axis_index("ctx") % 2
    away = dot(of_core(left, 1 - core), right, contract, bf16)
    arrived = swap(away, 1, count)
    stay = of_core(left, core)
    stay = after(stay, away, *wait)
    pairs = (dot(stay, right, contract) + arrived.astype(f32)).astype(bf16)
    return pairs.reshape(count // 2, -1, pairs.shape[1])


def scatter_pairs(pairs):
    count = lax.axis_size("ctx")
    bits = chip_bits()
    half, depth = pairs.shape[1] // 2, pairs.shape[2]
    pairs = pairs.reshape((2,) * len(bits) + (2, half, depth))
    sums = []
    for which in range(2):
        current = pairs[..., which, :, :]
        order = range(len(bits)) if which == 0 else range(len(bits) - 1, -1, -1)
        for at in order:
            step, bit = bits[at]
            axis = len(bits) - 1 - at
            away = lax.dynamic_slice_in_dim(current, 1 - bit, 1, axis).astype(bf16)
            stay = lax.dynamic_slice_in_dim(current, bit, 1, axis).astype(f32)
            current = stay + swap(away, step, count).astype(f32)
        sums.append(current.reshape(half, depth))
    return jnp.concatenate(sums)


def gather_seq(value):
    return lax.all_gather(value, "seq", axis=0, tiled=True)


def scatter_seq(value):
    return lax.psum_scatter(value, "seq", scatter_dimension=0, tiled=True)


def exchange_ctx(value):
    return lax.all_to_all(value, "ctx", 0, 0)


def gather_small(gains, segments):
    seqs, ranks = lax.axis_size("seq"), lax.axis_size("ctx")
    line = jnp.concatenate([part.astype(f32) for part in gains] + [segments[0].astype(f32)])
    spread = jnp.broadcast_to(line[None, None], (seqs * ranks, 1, line.shape[0]))
    table = lax.all_to_all(spread, BOTH, 0, 0)[:, 0]
    width = gains[0].shape[0]
    own = lax.dynamic_slice_in_dim(table, lax.axis_index("seq") * ranks, ranks, 0)
    return (
        table[:, :width].reshape(1, -1),
        table[:, width : 2 * width].reshape(1, -1),
        own[:, 2 * width :].reshape(1, -1),
    )


def split_kernel(seqs, ranks, units, gate_ref, up_ref, out_ref):
    for rank in range(ranks):
        for at, ref in enumerate((gate_ref, up_ref)):
            for seq in range(seqs):
                first = (seq * ranks + rank) * units
                to = (at * seqs + seq) * units
                out_ref[rank, :, to : to + units] = ref[:, first : first + units]


def split_units(gate, up, units):
    seqs, ranks = lax.axis_size("seq"), lax.axis_size("ctx")
    return pl.pallas_call(
        functools.partial(split_kernel, seqs, ranks, units),
        out_shape=jax.ShapeDtypeStruct((ranks, gate.shape[0], 2 * seqs * units), gate.dtype),
        compiler_params=pltpu.CompilerParams(vmem_limit_bytes=48 * 1024 * 1024),
        name="split_units",
    )(gate, up)


def join_kernel(
    seqs, ranks, units, grad_ref, gate_ref, up_ref, grad_gate_ref, grad_up_ref, sum_ref
):
    for at, ref in enumerate((grad_gate_ref, grad_up_ref)):
        for rank in range(ranks):
            for seq in range(seqs):
                first = (seq * ranks + rank) * units
                to = (at * seqs + seq) * units
                ref[:, first : first + units] = grad_ref[rank, :, to : to + units].astype(f32)
    terms = grad_gate_ref[...] * gate_ref[...].astype(f32)
    terms = terms + grad_up_ref[...] * up_ref[...].astype(f32)
    sum_ref[...] = jnp.sum(terms, axis=1, keepdims=True)


def join_units(grad, gate, up, units):
    seqs, ranks = lax.axis_size("seq"), lax.axis_size("ctx")
    whole = jax.ShapeDtypeStruct(gate.shape, f32)
    return pl.pallas_call(
        functools.partial(join_kernel, seqs, ranks, units),
        out_shape=[whole, whole, jax.ShapeDtypeStruct((gate.shape[0], 1), f32)],
        compiler_params=pltpu.CompilerParams(vmem_limit_bytes=48 * 1024 * 1024),
        name="join_units",
    )(grad, gate, up)


def forward_kernel(block, heads, key_ref, value_ref, query_ref, start_ref, out_ref, out_n_ref, lse_ref):
    at = pl.program_id(0)
    start = start_ref[...]
    rows = lax.broadcasted_iota(jnp.int32, (block, block), 0)
    columns = lax.broadcasted_iota(jnp.int32, (block, block), 1)

    out_ref[...] = jnp.zeros_like(out_ref)

    def step(j, carry, diagonal):
        first = pl.multiple_of(j * block, block)
        keys = key_ref[pl.ds(first, block), :]
        values = value_ref[:, pl.ds(first, block)]
        allowed = rows >= start - first
        if diagonal:
            allowed = allowed & (rows <= columns)
        fresh = []
        for head in range(heads):
            top, mass = carry[head]
            span = slice(head * HD, (head + 1) * HD)
            scores = dot(keys, query_ref[span, :], ((1,), (0,)))
            scores = jnp.where(allowed, scores, MASKED)
            high = jnp.maximum(top, jnp.max(scores, axis=0, keepdims=True))
            weights = jnp.exp(scores - high)
            fade = jnp.exp(top - high)
            mass = mass * fade + jnp.sum(weights, axis=0, keepdims=True)
            mixed = dot(values, weights.astype(bf16), ((1,), (0,)))
            out_ref[span, :] = out_ref[span, :] * fade + mixed
            fresh.append((high, mass))
        return tuple(fresh)

    begin = tuple(
        (jnp.full((1, block), MASKED, f32), jnp.zeros((1, block), f32)) for _ in range(heads)
    )
    carry = lax.fori_loop(0, at, lambda j, c: step(j, c, False), begin)
    carry = step(at, carry, True)
    for head in range(heads):
        top, mass = carry[head]
        span = slice(head * HD, (head + 1) * HD)
        out = out_ref[span, :] / mass
        out_ref[span, :] = out
        out_n_ref[:, span] = out.T.astype(bf16)
        lse_ref[head : head + 1, :] = top + jnp.log(mass)


def attention_forward(query_t, key_n, value_t, start, block):
    width, length = query_t.shape
    heads = width // HD
    return pl.pallas_call(
        functools.partial(forward_kernel, block, heads),
        grid=(length // block,),
        in_specs=[
            pl.BlockSpec((length, HD), lambda i: (0, 0)),
            pl.BlockSpec((HD, length), lambda i: (0, 0)),
            pl.BlockSpec((width, block), lambda i: (0, i)),
            pl.BlockSpec((1, block), lambda i: (0, i)),
        ],
        out_specs=[
            pl.BlockSpec((width, block), lambda i: (0, i)),
            pl.BlockSpec((block, width), lambda i: (i, 0)),
            pl.BlockSpec((heads, block), lambda i: (0, i)),
        ],
        out_shape=[
            jax.ShapeDtypeStruct((width, length), f32),
            jax.ShapeDtypeStruct((length, width), bf16),
            jax.ShapeDtypeStruct((heads, length), f32),
        ],
        compiler_params=pltpu.CompilerParams(vmem_limit_bytes=48 * 1024 * 1024),
        name="attention_forward",
    )(key_n, value_t, query_t, start)


def backward_kernel(
    block,
    heads,
    count,
    key_ref,
    key_t_ref,
    value_ref,
    query_ref,
    grad_ref,
    out_ref,
    lse_ref,
    start_ref,
    grad_query_ref,
    grad_key_ref,
    grad_value_ref,
    query_n,
    grad_n,
    delta,
    key_sum,
    value_sum,
):
    at = pl.program_id(0)
    rows = lax.broadcasted_iota(jnp.int32, (block, block), 0)
    columns = lax.broadcasted_iota(jnp.int32, (block, block), 1)

    @pl.when(at == 0)
    def _():
        grad_query_ref[...] = jnp.zeros_like(grad_query_ref)

        def turn(i, unused):
            part = pl.ds(pl.multiple_of(i * block, block), block)
            for head in range(heads):
                span = slice(head * HD, (head + 1) * HD)
                grads = grad_ref[span, part].astype(f32)
                query_n[head, part, :] = query_ref[span, part].astype(f32).T.astype(bf16)
                grad_n[head, part, :] = grads.T.astype(bf16)
                delta[head : head + 1, part] = jnp.sum(
                    grads * out_ref[span, part], axis=0, keepdims=True
                )
            return unused

        lax.fori_loop(0, count, turn, 0)

    key_sum[...] = jnp.zeros_like(key_sum)
    value_sum[...] = jnp.zeros_like(value_sum)
    keys = key_ref[...]
    keys_t = key_t_ref[...]
    values = value_ref[...]

    def step(i, diagonal):
        part = pl.ds(pl.multiple_of(i * block, block), block)
        allowed = rows >= start_ref[:, part] - at * block
        if diagonal:
            allowed = allowed & (rows <= columns)
        for head in range(heads):
            span = slice(head * HD, (head + 1) * HD)
            scores = dot(keys, query_ref[span, part], ((1,), (0,)))
            scores = jnp.where(allowed, scores, MASKED)
            probs = jnp.exp(scores - lse_ref[head : head + 1, part])
            value_sum[...] += dot(probs.astype(bf16), grad_n[head, part, :], ((1,), (0,)))
            grad_probs = dot(values, grad_ref[span, part], ((1,), (0,)))
            grad_scores = (probs * (grad_probs - delta[head : head + 1, part])).astype(bf16)
            key_sum[...] += dot(grad_scores, query_n[head, part, :], ((1,), (0,)))
            grad_query_ref[span, part] += dot(keys_t, grad_scores, ((1,), (0,)))

    step(at, True)

    def loop(i, unused):
        step(i, False)
        return unused

    lax.fori_loop(at + 1, count, loop, 0)
    grad_key_ref[...] = key_sum[...].T
    grad_value_ref[...] = value_sum[...].T


def attention_backward(query_t, key_n, key_t, value_n, grad_t, out_t, lse, start, block):
    width, length = query_t.shape
    heads = width // HD
    count = length // block
    whole = lambda j: (0, 0)
    return pl.pallas_call(
        functools.partial(backward_kernel, block, heads, count),
        grid=(count,),
        in_specs=[
            pl.BlockSpec((block, HD), lambda j: (j, 0)),
            pl.BlockSpec((HD, block), lambda j: (0, j)),
            pl.BlockSpec((block, HD), lambda j: (j, 0)),
            pl.BlockSpec((width, length), whole),
            pl.BlockSpec((width, length), whole),
            pl.BlockSpec((width, length), whole),
            pl.BlockSpec((heads, length), whole),
            pl.BlockSpec((1, length), whole),
        ],
        out_specs=[
            pl.BlockSpec((width, length), whole),
            pl.BlockSpec((HD, block), lambda j: (0, j)),
            pl.BlockSpec((HD, block), lambda j: (0, j)),
        ],
        out_shape=[
            jax.ShapeDtypeStruct((width, length), f32),
            jax.ShapeDtypeStruct((HD, length), f32),
            jax.ShapeDtypeStruct((HD, length), f32),
        ],
        scratch_shapes=[
            pltpu.VMEM((heads, length, HD), bf16),
            pltpu.VMEM((heads, length, HD), bf16),
            pltpu.VMEM((heads, length), f32),
            pltpu.VMEM((block, HD), f32),
            pltpu.VMEM((block, HD), f32),
        ],
        compiler_params=pltpu.CompilerParams(vmem_limit_bytes=48 * 1024 * 1024),
        name="attention_backward",
    )(key_n, key_t, value_n, query_t, grad_t, out_t, lse, start)


def rotate(source, cosine, sine_part):
    halves = source.reshape(-1, 2, HALF, source.shape[1])
    first, second = halves[:, 0], halves[:, 1]
    turned = jnp.stack(
        [first * cosine - second * sine_part, second * cosine + first * sine_part], axis=1
    )
    return turned.reshape(source.shape)


def body(
    tokens,
    segments,
    cotangent,
    attention_gain,
    query_weight,
    key_weight,
    value_weight,
    projection,
    feedforward_gain,
    gate_weight,
    up_weight,
    down_weight,
):
    seqs, ranks = lax.axis_size("seq"), lax.axis_size("ctx")
    rows = query_weight.shape[0]
    depth = tokens.shape[1]
    units = down_weight.shape[0]
    local_count = tokens.shape[0]
    length = local_count * ranks
    block = 256 if length % 256 == 0 else local_count
    width = H * HD // ranks

    def row_factor(values):
        return lax.rsqrt(jnp.mean(values * values, axis=-1, keepdims=True) + EPSILON)

    gain_one_row, gain_two_row, seg_row = gather_small(
        (attention_gain, feedforward_gain), segments
    )
    inputs = tokens.astype(f32)
    factor_one = row_factor(inputs)
    normed = (inputs * factor_one * gain_one_row).astype(bf16)

    def split_heads(weight):
        return jnp.repeat(weight.reshape(rows, KV, HD), ranks // KV, axis=1)

    mix = jnp.concatenate(
        [
            query_weight.reshape(rows, ranks, width),
            split_heads(key_weight),
            split_heads(value_weight),
        ],
        axis=2,
    ).transpose(1, 0, 2)
    mix = exchange_ctx(after(mix, seg_row)).reshape(ranks * rows, -1)
    mix_wide = gather_seq(mix)
    normed_all = gather_ctx(normed)
    index = [(i, (i % seqs) * ranks + i // seqs) for i in range(seqs * ranks)]
    proj_wide = gather_seq(after(lax.ppermute(projection, BOTH, index), mix))
    pair = split_units(after(gate_weight, mix), up_weight, units)
    pair = exchange_ctx(pair).reshape(ranks * rows, -1)
    pair_wide = gather_seq(after(pair, proj_wide))
    down_wide = gather_seq(after(down_weight, pair))
    hidden_units = units * seqs

    start = jnp.sum((seg_row < seg_row.T).astype(jnp.int32), axis=1)
    positions = jnp.arange(length, dtype=jnp.int32) - start
    freqs = jnp.power(10000.0, -jnp.arange(HALF, dtype=f32) * (2.0 / HD))
    angles = freqs[:, None] * positions.astype(f32)[None, :]
    cosine, sine_part = jnp.cos(angles), jnp.sin(angles)
    start_row = start[None, :]

    mixed = dot(mix_wide, normed_all, ((0,), (1,)))
    query_t = rotate(mixed[:width], cosine, sine_part).astype(bf16) * bf16(HD**-0.5)
    key_t = rotate(mixed[width : width + HD], cosine, sine_part).astype(bf16)
    value_t = mixed[width + HD :].astype(bf16)
    query_t = after(query_t, pair)
    key_n, value_n = key_t.T, value_t.T
    out_t, out_low, lse = attention_forward(query_t, key_n, value_t, start_row, block)
    cotangent_all = gather_ctx(after(cotangent, query_t))
    rows_by = ((1,), (0,))
    hidden = inputs + scatter_pairs(pair_up(out_low, proj_wide, rows_by))

    factor_two = row_factor(hidden)
    normed_two = (hidden * factor_two * gain_two_row).astype(bf16)
    normed_two_all = gather_ctx(normed_two)
    both = dot(normed_two_all, pair_wide, ((1,), (0,)))
    gate, upward = both[:, :hidden_units], both[:, hidden_units:]
    sigmoid_gate = jax.nn.sigmoid(gate)
    swished = gate * sigmoid_gate
    activated = (swished * upward).astype(bf16)
    grad_down = dot(activated, cotangent_all, ((0,), (0,)), bf16)
    grad_act = dot(cotangent_all, down_wide, ((1,), (1,)))
    grad_pair_in = jnp.concatenate(
        [
            (grad_act * upward * sigmoid_gate * (1.0 + gate * (1.0 - sigmoid_gate))).astype(bf16),
            (grad_act * swished).astype(bf16),
        ],
        axis=1,
    )
    grad_pair_in = after(grad_pair_in, grad_down)
    grad_down = scatter_seq(grad_down).astype(f32)
    columns_by = ((1,), (1,))
    shaped_two = scatter_pairs(pair_up(grad_pair_in, pair_wide, columns_by)) * gain_two_row
    grad_pair = dot(normed_two_all, grad_pair_in, ((0,), (0,)), bf16)
    shaped_two = after(shaped_two, grad_pair)
    grad_pair = scatter_seq(grad_pair)
    mean_two = jnp.mean(shaped_two * hidden, axis=-1, keepdims=True)
    grad_hidden = (
        cotangent.astype(f32)
        + factor_two * shaped_two
        - hidden * (factor_two * factor_two * factor_two * mean_two)
    )

    branch_all = gather_ctx(grad_hidden.astype(bf16))
    grad_out_t = dot(proj_wide, branch_all, columns_by, bf16)
    grad_proj = dot(out_low, branch_all, ((0,), (0,)), bf16)
    out_pairs = pair_up(after(activated, grad_out_t), down_wide, rows_by)
    grad_out_t = after(grad_out_t, grad_proj, out_pairs, grad_down)
    grad_query_t, grad_key_t, grad_value_t = attention_backward(
        query_t, key_n, key_t, value_n, grad_out_t, out_t, lse, start_row, block
    )
    grad_mixed = jnp.concatenate(
        [
            rotate(grad_query_t * HD**-0.5, cosine, -sine_part),
            rotate(grad_key_t, cosine, -sine_part),
            grad_value_t,
        ],
        axis=0,
    ).astype(bf16)
    grad_projection = lax.ppermute(
        scatter_seq(after(grad_proj, grad_pair)), BOTH, [(b, a) for a, b in index]
    ).astype(f32)
    block_out = (hidden + scatter_pairs(after(out_pairs, grad_out_t))).astype(bf16)
    grad_mix = dot(normed_all, grad_mixed, ((0,), (1,)), bf16)
    grad_pair = exchange_ctx(after(grad_pair, grad_mixed).reshape(ranks, rows, -1))
    mixed_n = after(grad_mixed.T, grad_mix)
    shaped_one = pair_up(mixed_n, mix_wide, columns_by)
    grad_mix = scatter_seq(grad_mix)
    grad_gate, grad_up, grad_feedforward = join_units(grad_pair, gate_weight, up_weight, units)
    shaped_one = after(scatter_pairs(shaped_one), grad_gate, block_out)
    shaped_one = shaped_one * gain_one_row
    mean_one = jnp.mean(shaped_one * inputs, axis=-1, keepdims=True)
    grad_tokens = (
        grad_hidden
        + factor_one * shaped_one
        - inputs * (factor_one * factor_one * factor_one * mean_one)
    )

    def join_heads(part):
        part = part.reshape(KV, ranks // KV, rows, HD).astype(f32).sum(axis=1)
        return part.transpose(1, 0, 2).reshape(rows, -1)

    def row_sum(grad, weight):
        return jnp.sum(grad * weight.astype(f32), axis=1)

    grad_feedforward = grad_feedforward[:, 0] / feedforward_gain.astype(f32)

    grad_mix = exchange_ctx(grad_mix.reshape(ranks, rows, -1))
    grad_query = grad_mix[:, :, :width].transpose(1, 0, 2).reshape(rows, -1).astype(f32)
    grad_key = join_heads(grad_mix[:, :, width : width + HD])
    grad_value = join_heads(grad_mix[:, :, width + HD :])
    grad_attention = (
        row_sum(grad_query, query_weight)
        + row_sum(grad_key, key_weight)
        + row_sum(grad_value, value_weight)
    ) / attention_gain.astype(f32)
    return (
        block_out,
        grad_tokens,
        grad_attention,
        grad_query,
        grad_key,
        grad_value,
        grad_projection,
        grad_feedforward,
        grad_gate,
        grad_up,
        grad_down,
    )


def solution(mesh):
    rows, plain = P(BOTH, None), P(BOTH)
    return jax.shard_map(
        body,
        mesh=mesh,
        in_specs=(rows, P("seq", "ctx"), rows, plain, rows, rows, rows, rows, plain, rows, rows, rows),
        out_specs=(rows, rows, plain, rows, rows, rows, rows, plain, rows, rows, rows),
        check_vma=False,
    )
```

```python
import functools

import jax
import jax.numpy as jnp
from jax import lax
from jax.experimental import pallas as pl
from jax.experimental.pallas import tpu as pltpu
from jax.sharding import PartitionSpec as P

H = 32
KV = 4
HD = 64
HALF = HD // 2

EPSILON = 1e-05
MASKED = -1e30
BOTH = ("seq", "ctx")
f32 = jnp.float32
bf16 = jnp.bfloat16
LIGHT = pl.CostEstimate(flops=0, transcendentals=0, bytes_accessed=0)


def dot(left, right, contract, out=f32):
    return lax.dot_general(left, right, (contract, ((), ())), preferred_element_type=f32).astype(out)


def after(value, *others):
    return lax.optimization_barrier((value, *others))[0]


def swap(value, step, count):
    return lax.ppermute(value, "ctx", [(i, i ^ step) for i in range(count)])


def blank(shape, dtype):
    return pl.pallas_call(
        lambda out_ref: None,
        out_shape=jax.ShapeDtypeStruct(shape, dtype),
        out_specs=pl.BlockSpec(memory_space=pl.ANY),
        name="blank",
    )()


def chip_bits():
    me = lax.axis_index("ctx")
    count = lax.axis_size("ctx")
    bits = [1 << at for at in range(1, count.bit_length() - 1)]
    return [(step, (me // step) % 2) for step in bits]


def gather_first(value):
    count = lax.axis_size("ctx")
    bits = chip_bits()
    half = value.shape[0] // 2
    steps = (bits[0][0], bits[-1][0])
    parts = [value[:half], value[half:]]
    return [(part, swap(part, step, count)) for part, step in zip(parts, steps)]


def gather_second(first):
    count = lax.axis_size("ctx")
    bits = chip_bits()
    parts = []
    for which, (current, arrived) in enumerate(first):
        half, depth = current.shape
        order = list(range(len(bits)))
        if which:
            order.reverse()
        current = current.reshape((1,) * len(bits) + (half, depth))
        arrived = arrived.reshape(current.shape)
        for at in order:
            step, bit = bits[at]
            axis = len(bits) - 1 - at
            if at != order[0]:
                arrived = swap(current, step, count)
            if at != order[-1]:
                current = jnp.where(
                    bit == 0,
                    jnp.concatenate([current, arrived], axis),
                    jnp.concatenate([arrived, current], axis),
                )
        parts.append((current, arrived))
    return parts


def place_kernel(bits, steps, natural, change, *refs):
    parts = 4 * 2
    given, gains = refs[:parts], refs[parts:-4]
    whole, held, ready, done = refs[-4:]
    me = lax.axis_index("ctx")
    core = lax.rem(me, 2)
    arrivals = [pltpu.make_async_copy(ref, held.at[i], ready.at[i]) for i, ref in enumerate(given)]
    copies = []
    for arrival in arrivals:
        arrival.start()
    for number, arrival in enumerate(arrivals):
        which, late, there = number // 4, number // 2 % 2, number % 2
        at = 0 if which else bits - 1
        axis = bits - 1 - at
        index = lax.rem(me // steps[at], 2)
        index = 1 - index if late else index
        owner = 1 - core if there else core
        spot = [slice(None)] * bits
        spot[axis] = index
        arrival.wait()
        if change is not None:
            held[number] = change(held[number], *[ref[...] for ref in gains])
        place = (*spot, owner, which) if natural else (there, *spot, which)
        copy = pltpu.make_async_copy(held.at[number], whole.at[place], done.at[number])
        copy.start()
        copies.append(copy)
    for copy in copies:
        copy.wait()


def gather_place(parts, natural=True, change=None, gains=()):
    count = lax.axis_size("ctx")
    steps = tuple(step for step, _ in chip_bits())
    half, depth = parts[0][0].shape[-2:]
    pieces = []
    for pair in parts:
        for part in pair:
            pieces += [part, swap(part, 1, count)]
    pieces = [piece.reshape((2,) * (len(steps) - 1) + (half, depth)) for piece in pieces]
    anywhere = pl.BlockSpec(memory_space=pl.ANY)
    dtype = pieces[0].dtype
    whole = pl.pallas_call(
        functools.partial(place_kernel, len(steps), steps, natural, change),
        in_specs=[anywhere] * len(pieces) + [pl.BlockSpec(memory_space=pltpu.VMEM)] * len(gains),
        out_specs=anywhere,
        out_shape=jax.ShapeDtypeStruct((2,) * len(steps) + (2, 2, half, depth), dtype),
        scratch_shapes=[
            pltpu.VMEM((len(pieces),) + pieces[0].shape, dtype),
            pltpu.SemaphoreType.DMA((len(pieces),)),
            pltpu.SemaphoreType.DMA((len(pieces),)),
        ],
        compiler_params=pltpu.CompilerParams(vmem_limit_bytes=48 * 1024 * 1024),
        cost_estimate=LIGHT,
        name="place",
    )(*pieces, *gains)
    return whole.reshape(2 * count * half, depth)


def send_chips(value):
    count = lax.axis_size("ctx")
    return {step: swap(value, step, count) if step else value for step in range(0, count, 2)}


def place_chips(pieces, natural=True):
    count = lax.axis_size("ctx")
    me = lax.axis_index("ctx")
    whole = blank((count,) + pieces[0].shape, pieces[0].dtype)
    for step, piece in pieces.items():
        for there in range(2):
            spot = me ^ step ^ there if natural else there * (count // 2) + (me ^ step) // 2
            piece = swap(piece, 1, count) if there else piece
            whole = lax.dynamic_update_index_in_dim(whole, piece, spot, 0)
    return whole.reshape((-1,) + pieces[0].shape[1:])


def double(value, step):
    seqs = lax.axis_size("seq")
    bit = (lax.axis_index("seq") // step) % 2
    other = lax.ppermute(value, "seq", [(i, i ^ step) for i in range(seqs)])
    whole = jnp.where(bit == 0, jnp.concatenate([value, other]), jnp.concatenate([other, value]))
    return whole, other


def double_to(value, end):
    step, other = 1, value
    while step < end:
        value, other = double(value, step)
        step *= 2
    return value, other


def head_order():
    seqs, ranks = lax.axis_size("seq"), lax.axis_size("ctx")
    return [(i, (i % seqs) * ranks + i // seqs) for i in range(seqs * ranks)]


def of_core(value, core):
    count = lax.axis_size("ctx")
    blocks = value.reshape(count // 2, 2, value.shape[0] // count, value.shape[1])
    return lax.dynamic_index_in_dim(blocks, core, 1, keepdims=False).reshape(-1, value.shape[1])


def blocks_of(pairs):
    return pairs.reshape(lax.axis_size("ctx") // 2, -1, pairs.shape[1])


def pair_up(left, right, contract):
    core = lax.axis_index("ctx") % 2
    away = dot(of_core(left, 1 - core), right, contract, bf16)
    arrived = swap(away, 1, lax.axis_size("ctx"))
    stay = after(of_core(left, core), away)
    return blocks_of((dot(stay, right, contract) + arrived.astype(f32)).astype(bf16))


def scatter_step(current, at):
    step, bit = chip_bits()[at]
    axis = current.ndim - 3 - at
    away = lax.dynamic_slice_in_dim(current, 1 - bit, 1, axis).astype(bf16)
    stay = lax.dynamic_slice_in_dim(current, bit, 1, axis).astype(f32)
    return stay, swap(away, step, lax.axis_size("ctx"))


def scatter_first(pairs):
    bits = len(chip_bits())
    half, depth = pairs.shape[1] // 2, pairs.shape[2]
    pairs = pairs.reshape((2,) * bits + (2, half, depth))
    return scatter_step(pairs[..., 0, :, :], 0), scatter_step(pairs[..., 1, :, :], bits - 1)


def scatter_rest(first):
    bits = len(chip_bits())
    low, high = first
    for at in range(1, bits):
        low = scatter_step(low[0] + low[1].astype(f32), at)
        high = scatter_step(high[0] + high[1].astype(f32), bits - 1 - at)
    sums = [stay + arrived.astype(f32) for stay, arrived in (low, high)]
    return jnp.concatenate([part.reshape(part.shape[-2:]) for part in sums])


def scatter_pairs(pairs):
    return scatter_rest(scatter_first(pairs))


def gather_seq(value):
    return lax.all_gather(value, "seq", axis=0, tiled=True)


def scatter_seq(value):
    return lax.psum_scatter(value, "seq", scatter_dimension=0, tiled=True)


def exchange_ctx(value):
    return lax.all_to_all(value, "ctx", 0, 0)


def gather_small(spread, segments):
    seqs, ranks = lax.axis_size("seq"), lax.axis_size("ctx")
    me = lax.axis_index("ctx")
    line = jnp.concatenate([spread.reshape(1, -1), segments.astype(f32)], axis=1)
    chips = send_chips(line)
    others = {step: swap(piece, 1, ranks) for step, piece in chips.items()}
    table = jnp.zeros((ranks, line.shape[1]), f32)
    for step, piece in chips.items():
        table = lax.dynamic_update_slice_in_dim(table, piece, me ^ step, 0)
        table = lax.dynamic_update_slice_in_dim(table, others[step], me ^ step ^ 1, 0)
    width = spread.size
    gains = table[:, :width].reshape(ranks, seqs, 2, -1).transpose(2, 1, 0, 3).reshape(2, -1)
    return gains[:1], gains[1:], table[:, width:].reshape(1, -1), list(others.values())


def unit_pieces(seqs, ranks, units):
    wide = seqs * units
    main = wide // 128 * 128
    for rank in range(ranks):
        for which in range(2):
            for seq in range(seqs):
                first, at, end = (seq * ranks + rank) * units, seq * units, (seq + 1) * units
                if at < main:
                    yield rank, which, first, which * main + at, min(end, main) - at
                if end > main:
                    cut = max(at, main)
                    to = 2 * main + which * (wide - main) + cut - main
                    yield rank, which, first + cut - at, to, end - cut


def split_kernel(pieces, gate_ref, up_ref, out_ref):
    refs = (gate_ref, up_ref)
    for rank, which, first, to, size in pieces:
        out_ref[rank, :, to : to + size] = refs[which][:, first : first + size]


def split_units(gate, up, units):
    seqs, ranks = lax.axis_size("seq"), lax.axis_size("ctx")
    return pl.pallas_call(
        functools.partial(split_kernel, tuple(unit_pieces(seqs, ranks, units))),
        out_shape=jax.ShapeDtypeStruct((ranks, gate.shape[0], 2 * seqs * units), gate.dtype),
        compiler_params=pltpu.CompilerParams(vmem_limit_bytes=48 * 1024 * 1024),
        name="split_units",
    )(gate, up)


def join_kernel(pieces, grad_ref, gate_ref, up_ref, grad_gate_ref, grad_up_ref, sum_ref):
    refs = (grad_gate_ref, grad_up_ref)
    for rank, which, first, to, size in pieces:
        refs[which][:, first : first + size] = grad_ref[rank, :, to : to + size].astype(f32)
    terms = grad_gate_ref[...] * gate_ref[...].astype(f32)
    terms = terms + grad_up_ref[...] * up_ref[...].astype(f32)
    sum_ref[...] = jnp.sum(terms, axis=1, keepdims=True)


def join_units(grad, gate, up, units):
    seqs, ranks = lax.axis_size("seq"), lax.axis_size("ctx")
    whole = jax.ShapeDtypeStruct(gate.shape, f32)
    return pl.pallas_call(
        functools.partial(join_kernel, tuple(unit_pieces(seqs, ranks, units))),
        out_shape=[whole, whole, jax.ShapeDtypeStruct((gate.shape[0], 1), f32)],
        compiler_params=pltpu.CompilerParams(vmem_limit_bytes=48 * 1024 * 1024),
        name="join_units",
    )(grad, gate, up)


def spans_of(hidden):
    main = hidden // 128 * 128
    return [(0, main)] + ([(main, hidden - main)] if main < hidden else [])


def units_kernel(hidden, row_ref, weight_ref, out_ref, slope_ref, swished_ref):
    both = dot(row_ref[...], weight_ref[...], ((1,), (0,)))
    for first, size in spans_of(hidden):
        span = slice(first, first + size)
        gate = both[:, 2 * first : 2 * first + size]
        upward = both[:, 2 * first + size : 2 * first + 2 * size]
        sigmoid_gate = jax.nn.sigmoid(gate)
        swished = gate * sigmoid_gate
        out_ref[:, span] = (swished * upward).astype(bf16)
        slope_ref[:, span] = (upward * sigmoid_gate * (1.0 + gate * (1.0 - sigmoid_gate))).astype(bf16)
        swished_ref[:, span] = swished.astype(bf16)


def units_back_kernel(hidden, grad_ref, down_ref, slope_ref, swished_ref, weight_ref, *refs):
    *given, out_ref, product_ref = refs
    grads = dot(grad_ref[...], down_ref[...], ((1,), (1,)))
    for first, size in spans_of(hidden):
        span = slice(first, first + size)
        grad = grads[:, span]
        out_ref[:, 2 * first : 2 * first + size] = (grad * slope_ref[:, span].astype(f32)).astype(bf16)
        out_ref[:, 2 * first + size : 2 * first + 2 * size] = (
            grad * swished_ref[:, span].astype(f32)
        ).astype(bf16)
    product = dot(out_ref[...], weight_ref[...], ((1,), (1,)))
    for ref in given:
        product = product + ref[...].astype(f32)
    product_ref[...] = product.astype(bf16)


def product_kernel(contract, row_ref, weight_ref, *refs):
    out = dot(row_ref[...], weight_ref[...], contract)
    for ref in refs[:-1]:
        out = out + ref[...].astype(f32)
    refs[-1][...] = out.astype(bf16)


def by_rows(kernel, rows, weight, widths, name, part=None, also=None):
    number, parts = part or (0, 1)
    count = rows[0].shape[0] // parts
    block = 256 if count % 256 == 0 else count

    def spec(array):
        first = number * (count // block) if array.shape[0] != count else 0
        return pl.BlockSpec((block, array.shape[1]), lambda i: (i + first, 0))

    arrays = list(rows)
    specs = [spec(array) for array in rows]
    for place, whole in ((1, weight), also or (0, None)):
        if whole is not None:
            arrays.insert(place, whole)
            specs.insert(place, pl.BlockSpec(whole.shape, lambda i: (0, 0)))
    return pl.pallas_call(
        kernel,
        grid=(count // block,),
        in_specs=specs,
        out_specs=[pl.BlockSpec((block, width), lambda i: (i, 0)) for width in widths],
        out_shape=[jax.ShapeDtypeStruct((count, width), bf16) for width in widths],
        compiler_params=pltpu.CompilerParams(vmem_limit_bytes=56 * 1024 * 1024),
        cost_estimate=LIGHT,
        name=name,
    )(*arrays)


def product(rows, weight, contract, part, name):
    kernel = functools.partial(product_kernel, contract)
    width = weight.shape[1 - contract[1][0]]
    return by_rows(kernel, rows, weight, [width], name, part)[0]


def attention_block(length):
    return 512 if length % 512 == 0 else length


def forward_kernel(
    block, heads, count, key_ref, value_ref, query_ref, start_ref, out_ref, out_n_ref, lse_ref
):
    def queries(at):
        end = (at + 1) * block
        rows = lax.broadcasted_iota(jnp.int32, (end, block), 0)
        columns = lax.broadcasted_iota(jnp.int32, (end, block), 1) + at * block
        allowed = (rows >= start_ref[...]) & (rows <= columns)
        for head in range(heads):
            span = slice(head * HD, (head + 1) * HD)
            scores = dot(key_ref[:end, :], query_ref[span, :], ((1,), (0,)))
            scores = jnp.where(allowed, scores, MASKED)
            top = jnp.max(scores, axis=0, keepdims=True)
            weights = jnp.exp(scores - top)
            mass = jnp.sum(weights, axis=0, keepdims=True)
            out = dot(value_ref[:, :end], weights.astype(bf16), ((1,), (0,))) / mass
            out_ref[span, :] = out
            out_n_ref[:, span] = out.T.astype(bf16)
            lse_ref[head : head + 1, :] = top + jnp.log(mass)

    for at in range(count):
        pl.when(pl.program_id(0) == at)(functools.partial(queries, at))


def attention_forward(query_t, key_n, value_t, start):
    width, length = query_t.shape
    heads = width // HD
    block = attention_block(length)
    return pl.pallas_call(
        functools.partial(forward_kernel, block, heads, length // block),
        grid=(length // block,),
        in_specs=[
            pl.BlockSpec((length, HD), lambda i: (0, 0)),
            pl.BlockSpec((HD, length), lambda i: (0, 0)),
            pl.BlockSpec((width, block), lambda i: (0, i)),
            pl.BlockSpec((1, block), lambda i: (0, i)),
        ],
        out_specs=[
            pl.BlockSpec((width, block), lambda i: (0, i)),
            pl.BlockSpec((block, width), lambda i: (i, 0)),
            pl.BlockSpec((heads, block), lambda i: (0, i)),
        ],
        out_shape=[
            jax.ShapeDtypeStruct((width, length), f32),
            jax.ShapeDtypeStruct((length, width), bf16),
            jax.ShapeDtypeStruct((heads, length), f32),
        ],
        compiler_params=pltpu.CompilerParams(vmem_limit_bytes=56 * 1024 * 1024),
        cost_estimate=LIGHT,
        name="attention_forward",
    )(key_n, value_t, query_t, start)


def backward_kernel(
    block,
    heads,
    count,
    key_ref,
    key_t_ref,
    value_ref,
    query_ref,
    grad_ref,
    out_ref,
    lse_ref,
    start_ref,
    grad_query_ref,
    grad_key_ref,
    grad_value_ref,
    query_n,
    grad_n,
    delta,
):
    spans = [slice(head * HD, (head + 1) * HD) for head in range(heads)]

    @pl.when(pl.program_id(0) == 0)
    def _():
        grad_query_ref[...] = jnp.zeros_like(grad_query_ref)
        for head, span in enumerate(spans):
            grads = grad_ref[span, :].astype(f32)
            query_n[head] = query_ref[span, :].astype(f32).T.astype(bf16)
            grad_n[head] = grads.T.astype(bf16)
            delta[head : head + 1, :] = jnp.sum(grads * out_ref[span, :], axis=0, keepdims=True)

    def keys(at):
        low = at * block
        shape = (block, (count - at) * block)
        rows = lax.broadcasted_iota(jnp.int32, shape, 0) + low
        columns = lax.broadcasted_iota(jnp.int32, shape, 1) + low
        allowed = (rows >= start_ref[:, low:]) & (rows <= columns)
        key_sum = jnp.zeros((block, HD), f32)
        value_sum = jnp.zeros((block, HD), f32)
        for head, span in enumerate(spans):
            scores = dot(key_ref[...], query_ref[span, low:], ((1,), (0,)))
            scores = jnp.where(allowed, scores, MASKED)
            probs = jnp.exp(scores - lse_ref[head : head + 1, low:])
            value_sum += dot(probs.astype(bf16), grad_n[head, low:, :], ((1,), (0,)))
            grad_probs = dot(value_ref[...], grad_ref[span, low:], ((1,), (0,)))
            grad_scores = (probs * (grad_probs - delta[head : head + 1, low:])).astype(bf16)
            key_sum += dot(grad_scores, query_n[head, low:, :], ((1,), (0,)))
            grad_query_ref[span, low:] += dot(key_t_ref[...], grad_scores, ((1,), (0,)))
        grad_key_ref[...] = key_sum.T
        grad_value_ref[...] = value_sum.T

    for at in range(count):
        pl.when(pl.program_id(0) == at)(functools.partial(keys, at))


def attention_backward(query_t, key_n, key_t, value_n, grad_t, out_t, lse, start):
    width, length = query_t.shape
    heads = width // HD
    block = attention_block(length)
    count = length // block

    def whole(j):
        return 0, 0

    return pl.pallas_call(
        functools.partial(backward_kernel, block, heads, count),
        grid=(count,),
        in_specs=[
            pl.BlockSpec((block, HD), lambda j: (j, 0)),
            pl.BlockSpec((HD, block), lambda j: (0, j)),
            pl.BlockSpec((block, HD), lambda j: (j, 0)),
            pl.BlockSpec((width, length), whole),
            pl.BlockSpec((width, length), whole),
            pl.BlockSpec((width, length), whole),
            pl.BlockSpec((heads, length), whole),
            pl.BlockSpec((1, length), whole),
        ],
        out_specs=[
            pl.BlockSpec((width, length), whole),
            pl.BlockSpec((HD, block), lambda j: (0, j)),
            pl.BlockSpec((HD, block), lambda j: (0, j)),
        ],
        out_shape=[
            jax.ShapeDtypeStruct((width, length), f32),
            jax.ShapeDtypeStruct((HD, length), f32),
            jax.ShapeDtypeStruct((HD, length), f32),
        ],
        scratch_shapes=[
            pltpu.VMEM((heads, length, HD), bf16),
            pltpu.VMEM((heads, length, HD), bf16),
            pltpu.VMEM((heads, length), f32),
        ],
        cost_estimate=pl.CostEstimate(flops=25_000_000_000, transcendentals=0, bytes_accessed=0),
        compiler_params=pltpu.CompilerParams(vmem_limit_bytes=56 * 1024 * 1024),
        name="attention_backward",
    )(key_n, key_t, value_n, query_t, grad_t, out_t, lse, start)


def rotate(source, cosine, sine_part):
    halves = source.reshape(-1, 2, HALF, source.shape[1])
    first, second = halves[:, 0], halves[:, 1]
    turned = jnp.stack(
        [first * cosine - second * sine_part, second * cosine + first * sine_part], axis=1
    )
    return turned.reshape(source.shape)


def body(
    tokens,
    segments,
    cotangent,
    attention_gain,
    query_weight,
    key_weight,
    value_weight,
    projection,
    feedforward_gain,
    gate_weight,
    up_weight,
    down_weight,
):
    seqs, ranks = lax.axis_size("seq"), lax.axis_size("ctx")
    rows = query_weight.shape[0]
    depth = tokens.shape[1]
    units = down_weight.shape[0]
    hidden_units = units * seqs
    local_count = tokens.shape[0]
    length = local_count * ranks
    width = H * HD // ranks

    def row_factor(values):
        return lax.rsqrt(jnp.mean(values * values, axis=-1, keepdims=True) + EPSILON)

    inputs = tokens.astype(f32)
    factor_one = row_factor(inputs)
    own_gains = jnp.concatenate([attention_gain, feedforward_gain]).astype(f32)[None]
    spread, last = double_to(own_gains, seqs)
    tokens_first = gather_first(tokens)

    def split_heads(weight):
        return jnp.repeat(weight.reshape(rows, KV, HD), ranks // KV, axis=1)

    mix = jnp.concatenate(
        [
            query_weight.reshape(rows, ranks, width),
            split_heads(key_weight),
            split_heads(value_weight),
        ],
        axis=2,
    ).transpose(1, 0, 2)
    gain_one_row, gain_two_row, seg_row, small = gather_small(spread, segments)
    mix = exchange_ctx(after(mix, last)).reshape(ranks * rows, -1)
    mix_wide = gather_seq(mix)
    tokens_second = gather_second(lax.optimization_barrier((tokens_first, mix))[0])
    pair = split_units(after(gate_weight, mix, *small), up_weight, units)
    pair = exchange_ctx(pair).reshape(ranks * rows, -1)
    proj = lax.ppermute(after(projection, mix), BOTH, head_order())
    proj_wide = gather_seq(proj)

    start = jnp.sum((seg_row < seg_row.T).astype(jnp.int32), axis=1)
    positions = jnp.arange(length, dtype=jnp.int32) - start
    freqs = jnp.power(10000.0, -jnp.arange(HALF, dtype=f32) * (2.0 / HD))
    angles = freqs[:, None] * positions.astype(f32)[None, :]
    cosine, sine_part = jnp.cos(angles), jnp.sin(angles)
    start_row = start[None, :]

    def normalize(piece, gain):
        piece = piece.astype(f32)
        return (piece * row_factor(piece) * gain).astype(bf16)

    normed_all = gather_place(tokens_second, True, normalize, (gain_one_row,))
    pair = after(pair, normed_all)
    pair_wide = gather_seq(pair)
    mixed = dot(mix_wide, normed_all, ((0,), (1,)))
    query_t = rotate(mixed[:width], cosine, sine_part).astype(bf16) * bf16(HD**-0.5)
    key_t = rotate(mixed[width : width + HD], cosine, sine_part).astype(bf16)
    value_t = mixed[width + HD :].astype(bf16)
    query_t = after(query_t, pair)
    key_n, value_n = key_t.T, value_t.T
    cotangent_pieces = send_chips(after(cotangent, normed_all))
    out_t, out_low, lse = attention_forward(query_t, key_n, value_t, start_row)
    out_low, cotangent_pieces = lax.optimization_barrier((out_low, cotangent_pieces))
    down_wide = gather_seq(after(down_weight, out_low))
    rows_by = ((1,), (0,))
    hidden = inputs + scatter_pairs(pair_up(out_low, proj_wide, rows_by))

    factor_two = row_factor(hidden)
    normed_two = (hidden * factor_two * gain_two_row).astype(bf16)
    cotangent_pieces, normed_two = lax.optimization_barrier((cotangent_pieces, normed_two))
    normed_two_first = gather_first(normed_two)
    cotangent_all = place_chips(cotangent_pieces, natural=False)
    columns_by = ((1,), (1,))
    normed_two_all = gather_place(gather_second(normed_two_first), natural=False)
    activated, slope, swished = by_rows(
        functools.partial(units_kernel, hidden_units),
        [normed_two_all],
        pair_wide,
        [hidden_units] * 3,
        "hidden_layer",
    )

    grad_down = dot(activated, cotangent_all, ((0,), (0,)), bf16)
    back = functools.partial(units_back_kernel, hidden_units)
    given = [after(cotangent_all, grad_down), slope, swished]
    wide = [2 * hidden_units, depth]
    both = (4, pair_wide)
    back_away, away = by_rows(back, given, down_wide, wide, "hidden_back_away", (1, 2), both)
    given[0] = after(given[0], away)
    given.append(swap(away, 1, ranks))
    back_stay, two_pairs = by_rows(back, given, down_wide, wide, "hidden_back_stay", (0, 2), both)
    two_pairs = blocks_of(two_pairs)
    grad_pair_in = jnp.concatenate([back_stay, back_away])
    grad_down = scatter_seq(grad_down).astype(f32)
    shaped_two = scatter_pairs(two_pairs) * gain_two_row
    grad_pair = dot(normed_two_all, grad_pair_in, ((0,), (0,)), bf16)
    shaped_two = after(shaped_two, grad_pair)
    grad_pair = scatter_seq(grad_pair)
    mean_two = jnp.mean(shaped_two * hidden, axis=-1, keepdims=True)
    grad_hidden = (
        cotangent.astype(f32)
        + factor_two * shaped_two
        - hidden * (factor_two * factor_two * factor_two * mean_two)
    )

    branch_first = gather_first(grad_hidden.astype(bf16))
    branch_second = gather_second(branch_first)
    activated = after(activated, shaped_two)
    away = product([activated], down_wide, rows_by, (1, 2), "out_away")
    given = [after(activated, away), swap(away, 1, ranks)]
    out_pairs = blocks_of(product(given, down_wide, rows_by, (0, 2), "out_stay"))
    branch_second, out_pairs = lax.optimization_barrier((branch_second, out_pairs))
    out_first = scatter_first(out_pairs)
    branch_all = gather_place(branch_second)
    grad_proj = dot(out_low, branch_all, ((0,), (0,)), bf16)
    grad_out_t = dot(proj_wide, branch_all, columns_by, bf16)
    grad_out_t, out_first, grad_down, grad_proj = lax.optimization_barrier(
        (grad_out_t, out_first, grad_down, grad_proj)
    )
    grad_out_t = after(grad_out_t, grad_pair)
    grad_proj = scatter_seq(grad_proj)
    out_sum = scatter_rest(out_first)
    grad_query_t, grad_key_t, grad_value_t = attention_backward(
        query_t, key_n, key_t, value_n, grad_out_t, out_t, lse, start_row
    )
    grad_mixed = jnp.concatenate(
        [
            rotate(grad_query_t * HD**-0.5, cosine, -sine_part),
            rotate(grad_key_t, cosine, -sine_part),
            grad_value_t,
        ],
        axis=0,
    ).astype(bf16)
    grad_pair = exchange_ctx(grad_pair.reshape(ranks, rows, -1))
    grad_mixed = after(grad_mixed, out_sum, grad_proj, grad_pair)
    block_out = (hidden + out_sum).astype(bf16)
    grad_mix = dot(normed_all, grad_mixed, ((0,), (1,)), bf16)
    mixed_n = after(grad_mixed.T, grad_mix)
    grad_mix = scatter_seq(grad_mix)
    shaped_one = pair_up(mixed_n, mix_wide, columns_by)
    grad_gate, grad_up, grad_feedforward = join_units(grad_pair, gate_weight, up_weight, units)
    shaped_first = scatter_first(shaped_one)
    arrived = [part for _, part in shaped_first]
    shaped_first, grad_gate, block_out = lax.optimization_barrier(
        (shaped_first, grad_gate, block_out)
    )
    shaped_one = scatter_rest(shaped_first)
    shaped_one = shaped_one * gain_one_row
    mean_one = jnp.mean(shaped_one * inputs, axis=-1, keepdims=True)
    grad_tokens = (
        grad_hidden
        + factor_one * shaped_one
        - inputs * (factor_one * factor_one * factor_one * mean_one)
    )

    def join_heads(part):
        part = part.reshape(KV, ranks // KV, rows, HD).astype(f32).sum(axis=1)
        return part.transpose(1, 0, 2).reshape(rows, -1)

    def row_sum(grad, weight):
        return jnp.sum(grad * weight.astype(f32), axis=1)

    grad_feedforward = grad_feedforward[:, 0] / feedforward_gain.astype(f32)

    grad_mix = exchange_ctx(after(grad_mix, *arrived).reshape(ranks, rows, -1))
    grad_query = grad_mix[:, :, :width].transpose(1, 0, 2).reshape(rows, -1).astype(f32)
    grad_key = join_heads(grad_mix[:, :, width : width + HD])
    grad_value = join_heads(grad_mix[:, :, width + HD :])
    grad_attention = (
        row_sum(grad_query, query_weight)
        + row_sum(grad_key, key_weight)
        + row_sum(grad_value, value_weight)
    ) / attention_gain.astype(f32)
    back_order = [(b, a) for a, b in head_order()]
    grad_projection = lax.ppermute(grad_proj, BOTH, back_order).astype(f32)
    return (
        block_out,
        grad_tokens,
        grad_attention,
        grad_query,
        grad_key,
        grad_value,
        grad_projection,
        grad_feedforward,
        grad_gate,
        grad_up,
        grad_down,
    )


def solution(mesh):
    rows, plain = P(BOTH, None), P(BOTH)
    return jax.shard_map(
        body,
        mesh=mesh,
        in_specs=(rows, P("seq", "ctx"), rows, plain, rows, rows, rows, rows, plain, rows, rows, rows),
        out_specs=(rows, rows, plain, rows, rows, rows, rows, plain, rows, rows, rows),
        check_vma=False,
    )
```

```python
import functools

import jax
import jax.numpy as jnp
from jax import lax
from jax.experimental import pallas as pl
from jax.experimental.pallas import tpu as pltpu
from jax.sharding import PartitionSpec as P

H = 32
KV = 4
HD = 64
HALF = HD // 2

EPSILON = 1e-05
MASKED = -1e30
BOTH = ("seq", "ctx")
f32 = jnp.float32
bf16 = jnp.bfloat16
LIGHT = pl.CostEstimate(flops=0, transcendentals=0, bytes_accessed=0)


def dot(left, right, contract, out=f32):
    return lax.dot_general(left, right, (contract, ((), ())), preferred_element_type=f32).astype(out)


def after(value, *others):
    return lax.optimization_barrier((value, *others))[0]


def swap(value, step, count):
    return lax.ppermute(value, "ctx", [(i, i ^ step) for i in range(count)])


def blank(shape, dtype):
    return pl.pallas_call(
        lambda out_ref: None,
        out_shape=jax.ShapeDtypeStruct(shape, dtype),
        out_specs=pl.BlockSpec(memory_space=pl.ANY),
        name="blank",
    )()


def chip_bits():
    me = lax.axis_index("ctx")
    count = lax.axis_size("ctx")
    bits = [1 << at for at in range(1, count.bit_length() - 1)]
    return [(step, (me // step) % 2) for step in bits]


def gather_first(value, beside=None):
    count = lax.axis_size("ctx")
    bits = chip_bits()
    half = value.shape[0] // 2
    steps = (bits[0][0], bits[-1][0])
    parts = [value[:half], value[half:]]
    if beside is not None:
        parts, beside = lax.optimization_barrier((parts, beside))
    first = [(part, swap(part, step, count)) for part, step in zip(parts, steps)]
    return first if beside is None else (first, beside)


def gather_second(first):
    count = lax.axis_size("ctx")
    bits = chip_bits()
    parts = []
    for which, (current, arrived) in enumerate(first):
        half, depth = current.shape
        order = list(range(len(bits)))
        if which:
            order.reverse()
        current = current.reshape((1,) * len(bits) + (half, depth))
        arrived = arrived.reshape(current.shape)
        for at in order:
            step, bit = bits[at]
            axis = len(bits) - 1 - at
            if at != order[0]:
                arrived = swap(current, step, count)
            if at != order[-1]:
                current = jnp.where(
                    bit == 0,
                    jnp.concatenate([current, arrived], axis),
                    jnp.concatenate([arrived, current], axis),
                )
        parts.append((current, arrived))
    return parts


def place_kernel(bits, steps, natural, change, *refs):
    parts = 4 * 2
    given, gains = refs[:parts], refs[parts:-4]
    whole, held, ready, done = refs[-4:]
    me = lax.axis_index("ctx")
    core = lax.rem(me, 2)
    arrivals = [pltpu.make_async_copy(ref, held.at[i], ready.at[i]) for i, ref in enumerate(given)]
    copies = []
    for arrival in arrivals:
        arrival.start()
    for number, arrival in enumerate(arrivals):
        which, late, there = number // 4, number // 2 % 2, number % 2
        at = 0 if which else bits - 1
        axis = bits - 1 - at
        index = lax.rem(me // steps[at], 2)
        index = 1 - index if late else index
        owner = 1 - core if there else core
        spot = [slice(None)] * bits
        spot[axis] = index
        arrival.wait()
        if change is not None:
            held[number] = change(held[number], *[ref[...] for ref in gains])
        place = (*spot, owner, which) if natural else (there, *spot, which)
        copy = pltpu.make_async_copy(held.at[number], whole.at[place], done.at[number])
        copy.start()
        copies.append(copy)
    for copy in copies:
        copy.wait()


def gather_place(parts, natural=True, change=None, gains=()):
    count = lax.axis_size("ctx")
    steps = tuple(step for step, _ in chip_bits())
    half, depth = parts[0][0].shape[-2:]
    pieces = []
    for pair in parts:
        for part in pair:
            pieces += [part, swap(part, 1, count)]
    pieces = [piece.reshape((2,) * (len(steps) - 1) + (half, depth)) for piece in pieces]
    anywhere = pl.BlockSpec(memory_space=pl.ANY)
    dtype = pieces[0].dtype
    whole = pl.pallas_call(
        functools.partial(place_kernel, len(steps), steps, natural, change),
        in_specs=[anywhere] * len(pieces) + [pl.BlockSpec(memory_space=pltpu.VMEM)] * len(gains),
        out_specs=anywhere,
        out_shape=jax.ShapeDtypeStruct((2,) * len(steps) + (2, 2, half, depth), dtype),
        scratch_shapes=[
            pltpu.VMEM((len(pieces),) + pieces[0].shape, dtype),
            pltpu.SemaphoreType.DMA((len(pieces),)),
            pltpu.SemaphoreType.DMA((len(pieces),)),
        ],
        compiler_params=pltpu.CompilerParams(vmem_limit_bytes=48 * 1024 * 1024),
        cost_estimate=LIGHT,
        name="place",
    )(*pieces, *gains)
    return whole.reshape(2 * count * half, depth)


def send_chips(value):
    count = lax.axis_size("ctx")
    return {step: swap(value, step, count) if step else value for step in range(0, count, 2)}


def place_chips(pieces, natural=True):
    count = lax.axis_size("ctx")
    me = lax.axis_index("ctx")
    whole = blank((count,) + pieces[0].shape, pieces[0].dtype)
    for step, piece in pieces.items():
        for there in range(2):
            spot = me ^ step ^ there if natural else there * (count // 2) + (me ^ step) // 2
            piece = swap(piece, 1, count) if there else piece
            whole = lax.dynamic_update_index_in_dim(whole, piece, spot, 0)
    return whole.reshape((-1,) + pieces[0].shape[1:])


def double(value, step):
    seqs = lax.axis_size("seq")
    bit = (lax.axis_index("seq") // step) % 2
    other = lax.ppermute(value, "seq", [(i, i ^ step) for i in range(seqs)])
    whole = jnp.where(bit == 0, jnp.concatenate([value, other]), jnp.concatenate([other, value]))
    return whole, other


def double_to(value, end):
    step, other = 1, value
    while step < end:
        value, other = double(value, step)
        step *= 2
    return value, other


def head_order():
    seqs, ranks = lax.axis_size("seq"), lax.axis_size("ctx")
    return [(i, (i % seqs) * ranks + i // seqs) for i in range(seqs * ranks)]


def to_owners(value):
    seqs, ranks = lax.axis_size("seq"), lax.axis_size("ctx")
    me = lax.axis_index("ctx")
    share = ranks // seqs
    blocks = value.reshape(seqs, -1, value.shape[1])
    whole = blank(blocks.shape, value.dtype)
    came = []
    for turn in range(seqs):
        piece = lax.dynamic_index_in_dim(blocks, (me // share + seqs - turn) % seqs, 0, False)
        pairs = [(r, r % share * seqs + (r // share - turn) % seqs) for r in range(ranks)]
        came.append(lax.ppermute(piece, "ctx", pairs))
        spot = (me % seqs + turn) % seqs
        whole = lax.dynamic_update_index_in_dim(whole, came[-1], spot, 0)
    return whole.reshape(value.shape), came


def of_core(value, core):
    count = lax.axis_size("ctx")
    blocks = value.reshape(count // 2, 2, value.shape[0] // count, value.shape[1])
    return lax.dynamic_index_in_dim(blocks, core, 1, keepdims=False).reshape(-1, value.shape[1])


def blocks_of(pairs):
    return pairs.reshape(lax.axis_size("ctx") // 2, -1, pairs.shape[1])


def pair_up(left, right, contract):
    core = lax.axis_index("ctx") % 2
    away = dot(of_core(left, 1 - core), right, contract, bf16)
    arrived = swap(away, 1, lax.axis_size("ctx"))
    stay = after(of_core(left, core), away)
    return blocks_of((dot(stay, right, contract) + arrived.astype(f32)).astype(bf16))


def scatter_parts(current, at):
    bit = chip_bits()[at][1]
    axis = current.ndim - 3 - at
    stay = lax.dynamic_slice_in_dim(current, bit, 1, axis).astype(f32)
    return stay, lax.dynamic_slice_in_dim(current, 1 - bit, 1, axis).astype(bf16)


def scatter_first(pairs, beside=()):
    count = lax.axis_size("ctx")
    bits = chip_bits()
    half, depth = pairs.shape[1] // 2, pairs.shape[2]
    pairs = pairs.reshape((2,) * len(bits) + (2, half, depth))
    low = scatter_parts(pairs[..., 0, :, :], 0)
    high = scatter_parts(pairs[..., 1, :, :], len(bits) - 1)
    aways, beside = lax.optimization_barrier(((low[1], high[1]), beside))
    first = [
        (stay, swap(away, bits[at][0], count))
        for (stay, _), away, at in ((low, aways[0], 0), (high, aways[1], len(bits) - 1))
    ]
    return first, beside


def scatter_rest(first):
    count = lax.axis_size("ctx")
    bits = chip_bits()
    last = []
    sums = []
    for which, (stay, arrived) in enumerate(first):
        for at in range(1, len(bits)):
            at = len(bits) - 1 - at if which else at
            stay, away = scatter_parts(stay + arrived.astype(f32), at)
            arrived = swap(away, bits[at][0], count)
        last.append(arrived)
        sums.append(stay + arrived.astype(f32))
    return jnp.concatenate([part.reshape(part.shape[-2:]) for part in sums]), last


def scatter_pairs(pairs):
    return scatter_rest(scatter_first(pairs)[0])[0]


def gather_seq(value):
    return lax.all_gather(value, "seq", axis=0, tiled=True)


def scatter_seq(value):
    return lax.psum_scatter(value, "seq", scatter_dimension=0, tiled=True)


def exchange_ctx(value):
    return lax.all_to_all(value, "ctx", 0, 0)


def gather_small(spread, segments):
    seqs, ranks = lax.axis_size("seq"), lax.axis_size("ctx")
    me = lax.axis_index("ctx")
    line = jnp.concatenate([spread.reshape(1, -1), segments.astype(f32)], axis=1)
    chips = send_chips(line)
    others = {step: swap(piece, 1, ranks) for step, piece in chips.items()}
    table = jnp.zeros((ranks, line.shape[1]), f32)
    for step, piece in chips.items():
        table = lax.dynamic_update_slice_in_dim(table, piece, me ^ step, 0)
        table = lax.dynamic_update_slice_in_dim(table, others[step], me ^ step ^ 1, 0)
    width = spread.size
    gains = table[:, :width].reshape(ranks, seqs, 2, -1).transpose(2, 1, 0, 3).reshape(2, -1)
    return gains[:1], gains[1:], table[:, width:].reshape(1, -1), list(others.values())


def unit_pieces(seqs, ranks, units):
    wide = seqs * units
    main = wide // 128 * 128
    for rank in range(ranks):
        for which in range(2):
            for seq in range(seqs):
                first, at, end = (seq * ranks + rank) * units, seq * units, (seq + 1) * units
                if at < main:
                    yield rank, which, first, which * main + at, min(end, main) - at
                if end > main:
                    cut = max(at, main)
                    to = 2 * main + which * (wide - main) + cut - main
                    yield rank, which, first + cut - at, to, end - cut


def split_kernel(pieces, gate_ref, up_ref, out_ref):
    refs = (gate_ref, up_ref)
    for rank, which, first, to, size in pieces:
        out_ref[rank, :, to : to + size] = refs[which][:, first : first + size]


def split_units(gate, up, units):
    seqs, ranks = lax.axis_size("seq"), lax.axis_size("ctx")
    return pl.pallas_call(
        functools.partial(split_kernel, tuple(unit_pieces(seqs, ranks, units))),
        out_shape=jax.ShapeDtypeStruct((ranks, gate.shape[0], 2 * seqs * units), gate.dtype),
        compiler_params=pltpu.CompilerParams(vmem_limit_bytes=48 * 1024 * 1024),
        name="split_units",
    )(gate, up)


def join_kernel(pieces, grad_ref, gate_ref, up_ref, grad_gate_ref, grad_up_ref, sum_ref):
    refs = (grad_gate_ref, grad_up_ref)
    for rank, which, first, to, size in pieces:
        refs[which][:, first : first + size] = grad_ref[rank, :, to : to + size].astype(f32)
    terms = grad_gate_ref[...] * gate_ref[...].astype(f32)
    terms = terms + grad_up_ref[...] * up_ref[...].astype(f32)
    sum_ref[...] = jnp.sum(terms, axis=1, keepdims=True)


def join_units(grad, gate, up, units):
    seqs, ranks = lax.axis_size("seq"), lax.axis_size("ctx")
    whole = jax.ShapeDtypeStruct(gate.shape, f32)
    return pl.pallas_call(
        functools.partial(join_kernel, tuple(unit_pieces(seqs, ranks, units))),
        out_shape=[whole, whole, jax.ShapeDtypeStruct((gate.shape[0], 1), f32)],
        compiler_params=pltpu.CompilerParams(vmem_limit_bytes=48 * 1024 * 1024),
        name="join_units",
    )(grad, gate, up)


def spans_of(hidden):
    main = hidden // 128 * 128
    return [(0, main)] + ([(main, hidden - main)] if main < hidden else [])


def units_kernel(hidden, row_ref, weight_ref, out_ref, slope_ref, swished_ref):
    both = dot(row_ref[...], weight_ref[...], ((1,), (0,)))
    for first, size in spans_of(hidden):
        span = slice(first, first + size)
        gate = both[:, 2 * first : 2 * first + size]
        upward = both[:, 2 * first + size : 2 * first + 2 * size]
        sigmoid_gate = jax.nn.sigmoid(gate)
        swished = gate * sigmoid_gate
        out_ref[:, span] = (swished * upward).astype(bf16)
        slope_ref[:, span] = (upward * sigmoid_gate * (1.0 + gate * (1.0 - sigmoid_gate))).astype(bf16)
        swished_ref[:, span] = swished.astype(bf16)


def units_back_kernel(hidden, grad_ref, down_ref, slope_ref, swished_ref, weight_ref, *refs):
    *given, out_ref, product_ref = refs
    grads = dot(grad_ref[...], down_ref[...], ((1,), (1,)))
    for first, size in spans_of(hidden):
        span = slice(first, first + size)
        grad = grads[:, span]
        out_ref[:, 2 * first : 2 * first + size] = (grad * slope_ref[:, span].astype(f32)).astype(bf16)
        out_ref[:, 2 * first + size : 2 * first + 2 * size] = (
            grad * swished_ref[:, span].astype(f32)
        ).astype(bf16)
    product = dot(out_ref[...], weight_ref[...], ((1,), (1,)))
    for ref in given:
        product = product + ref[...].astype(f32)
    product_ref[...] = product.astype(bf16)


def product_kernel(contract, row_ref, weight_ref, *refs):
    out = dot(row_ref[...], weight_ref[...], contract)
    for ref in refs[:-1]:
        out = out + ref[...].astype(f32)
    refs[-1][...] = out.astype(bf16)


def by_rows(kernel, rows, weight, widths, name, part=None, also=None, cost=LIGHT):
    number, parts = part or (0, 1)
    count = rows[0].shape[0] // parts
    block = 256 if count % 256 == 0 else count

    def spec(array):
        first = number * (count // block) if array.shape[0] != count else 0
        return pl.BlockSpec((block, array.shape[1]), lambda i: (i + first, 0))

    arrays = list(rows)
    specs = [spec(array) for array in rows]
    for place, whole in ((1, weight), also or (0, None)):
        if whole is not None:
            arrays.insert(place, whole)
            specs.insert(place, pl.BlockSpec(whole.shape, lambda i: (0, 0)))
    return pl.pallas_call(
        kernel,
        grid=(count // block,),
        in_specs=specs,
        out_specs=[pl.BlockSpec((block, width), lambda i: (i, 0)) for width in widths],
        out_shape=[jax.ShapeDtypeStruct((count, width), bf16) for width in widths],
        compiler_params=pltpu.CompilerParams(vmem_limit_bytes=56 * 1024 * 1024),
        cost_estimate=cost,
        name=name,
    )(*arrays)


def product(rows, weight, contract, part, name):
    kernel = functools.partial(product_kernel, contract)
    width = weight.shape[1 - contract[1][0]]
    cost = pl.CostEstimate(flops=7_000_000_000, transcendentals=0, bytes_accessed=0)
    return by_rows(kernel, rows, weight, [width], name, part, None, cost)[0]


def outer_kernel(row_ref, *refs):
    *others, out_ref = refs
    first, total = 0, 0.0
    for ref in others:
        end = first + ref.shape[0]
        total = total + dot(row_ref[first:end, :], ref[...], ((0,), (0,)))
        first = end
    out_ref[...] = total.astype(bf16)


def outer(row, others):
    count, depth = row.shape
    width = others[0].shape[1]
    block = 512 if depth % 512 == 0 else depth
    return pl.pallas_call(
        outer_kernel,
        grid=(depth // block,),
        in_specs=[pl.BlockSpec((count, block), lambda i: (0, i))]
        + [pl.BlockSpec(other.shape, lambda i: (0, 0)) for other in others],
        out_specs=pl.BlockSpec((block, width), lambda i: (i, 0)),
        out_shape=jax.ShapeDtypeStruct((depth, width), bf16),
        compiler_params=pltpu.CompilerParams(vmem_limit_bytes=56 * 1024 * 1024),
        cost_estimate=LIGHT,
        name="outer",
    )(row, *others)


def attention_block(length):
    return 512 if length % 512 == 0 else length


def forward_kernel(
    block, heads, count, key_ref, value_ref, query_ref, start_ref, out_ref, out_n_ref, lse_ref
):
    def queries(at):
        end = (at + 1) * block
        rows = lax.broadcasted_iota(jnp.int32, (end, block), 0)
        columns = lax.broadcasted_iota(jnp.int32, (end, block), 1) + at * block
        allowed = (rows >= start_ref[...]) & (rows <= columns)
        for head in range(heads):
            span = slice(head * HD, (head + 1) * HD)
            scores = dot(key_ref[:end, :], query_ref[span, :], ((1,), (0,)))
            scores = jnp.where(allowed, scores, MASKED)
            top = jnp.max(scores, axis=0, keepdims=True)
            weights = jnp.exp(scores - top)
            mass = jnp.sum(weights, axis=0, keepdims=True)
            out = dot(value_ref[:, :end], weights.astype(bf16), ((1,), (0,))) / mass
            out_ref[span, :] = out
            out_n_ref[:, span] = out.T.astype(bf16)
            lse_ref[head : head + 1, :] = top + jnp.log(mass)

    for at in range(count):
        pl.when(pl.program_id(0) == at)(functools.partial(queries, at))


def attention_forward(query_t, key_n, value_t, start):
    width, length = query_t.shape
    heads = width // HD
    block = attention_block(length)
    return pl.pallas_call(
        functools.partial(forward_kernel, block, heads, length // block),
        grid=(length // block,),
        in_specs=[
            pl.BlockSpec((length, HD), lambda i: (0, 0)),
            pl.BlockSpec((HD, length), lambda i: (0, 0)),
            pl.BlockSpec((width, block), lambda i: (0, i)),
            pl.BlockSpec((1, block), lambda i: (0, i)),
        ],
        out_specs=[
            pl.BlockSpec((width, block), lambda i: (0, i)),
            pl.BlockSpec((block, width), lambda i: (i, 0)),
            pl.BlockSpec((heads, block), lambda i: (0, i)),
        ],
        out_shape=[
            jax.ShapeDtypeStruct((width, length), f32),
            jax.ShapeDtypeStruct((length, width), bf16),
            jax.ShapeDtypeStruct((heads, length), f32),
        ],
        compiler_params=pltpu.CompilerParams(vmem_limit_bytes=56 * 1024 * 1024),
        cost_estimate=LIGHT,
        name="attention_forward",
    )(key_n, value_t, query_t, start)


def backward_kernel(
    block,
    heads,
    count,
    key_ref,
    key_t_ref,
    value_ref,
    query_ref,
    grad_ref,
    out_ref,
    lse_ref,
    start_ref,
    grad_query_ref,
    grad_key_ref,
    grad_value_ref,
    query_n,
    grad_n,
    delta,
):
    spans = [slice(head * HD, (head + 1) * HD) for head in range(heads)]

    @pl.when(pl.program_id(0) == 0)
    def _():
        grad_query_ref[...] = jnp.zeros_like(grad_query_ref)
        for head, span in enumerate(spans):
            grads = grad_ref[span, :].astype(f32)
            query_n[head] = query_ref[span, :].astype(f32).T.astype(bf16)
            grad_n[head] = grads.T.astype(bf16)
            delta[head : head + 1, :] = jnp.sum(grads * out_ref[span, :], axis=0, keepdims=True)

    def keys(at):
        low = at * block
        shape = (block, (count - at) * block)
        rows = lax.broadcasted_iota(jnp.int32, shape, 0) + low
        columns = lax.broadcasted_iota(jnp.int32, shape, 1) + low
        allowed = (rows >= start_ref[:, low:]) & (rows <= columns)
        key_sum = jnp.zeros((block, HD), f32)
        value_sum = jnp.zeros((block, HD), f32)
        for head, span in enumerate(spans):
            scores = dot(key_ref[...], query_ref[span, low:], ((1,), (0,)))
            scores = jnp.where(allowed, scores, MASKED)
            probs = jnp.exp(scores - lse_ref[head : head + 1, low:])
            value_sum += dot(probs.astype(bf16), grad_n[head, low:, :], ((1,), (0,)))
            grad_probs = dot(value_ref[...], grad_ref[span, low:], ((1,), (0,)))
            grad_scores = (probs * (grad_probs - delta[head : head + 1, low:])).astype(bf16)
            key_sum += dot(grad_scores, query_n[head, low:, :], ((1,), (0,)))
            grad_query_ref[span, low:] += dot(key_t_ref[...], grad_scores, ((1,), (0,)))
        grad_key_ref[...] = key_sum.T
        grad_value_ref[...] = value_sum.T

    for at in range(count):
        pl.when(pl.program_id(0) == at)(functools.partial(keys, at))


def attention_backward(query_t, key_n, key_t, value_n, grad_t, out_t, lse, start):
    width, length = query_t.shape
    heads = width // HD
    block = attention_block(length)
    count = length // block

    def whole(j):
        return 0, 0

    return pl.pallas_call(
        functools.partial(backward_kernel, block, heads, count),
        grid=(count,),
        in_specs=[
            pl.BlockSpec((block, HD), lambda j: (j, 0)),
            pl.BlockSpec((HD, block), lambda j: (0, j)),
            pl.BlockSpec((block, HD), lambda j: (j, 0)),
            pl.BlockSpec((width, length), whole),
            pl.BlockSpec((width, length), whole),
            pl.BlockSpec((width, length), whole),
            pl.BlockSpec((heads, length), whole),
            pl.BlockSpec((1, length), whole),
        ],
        out_specs=[
            pl.BlockSpec((width, length), whole),
            pl.BlockSpec((HD, block), lambda j: (0, j)),
            pl.BlockSpec((HD, block), lambda j: (0, j)),
        ],
        out_shape=[
            jax.ShapeDtypeStruct((width, length), f32),
            jax.ShapeDtypeStruct((HD, length), f32),
            jax.ShapeDtypeStruct((HD, length), f32),
        ],
        scratch_shapes=[
            pltpu.VMEM((heads, length, HD), bf16),
            pltpu.VMEM((heads, length, HD), bf16),
            pltpu.VMEM((heads, length), f32),
        ],
        cost_estimate=pl.CostEstimate(flops=25_000_000_000, transcendentals=0, bytes_accessed=0),
        compiler_params=pltpu.CompilerParams(vmem_limit_bytes=56 * 1024 * 1024),
        name="attention_backward",
    )(key_n, key_t, value_n, query_t, grad_t, out_t, lse, start)


def rotate(source, cosine, sine_part):
    halves = source.reshape(-1, 2, HALF, source.shape[1])
    first, second = halves[:, 0], halves[:, 1]
    turned = jnp.stack(
        [first * cosine - second * sine_part, second * cosine + first * sine_part], axis=1
    )
    return turned.reshape(source.shape)


def body(
    tokens,
    segments,
    cotangent,
    attention_gain,
    query_weight,
    key_weight,
    value_weight,
    projection,
    feedforward_gain,
    gate_weight,
    up_weight,
    down_weight,
):
    seqs, ranks = lax.axis_size("seq"), lax.axis_size("ctx")
    rows = query_weight.shape[0]
    depth = tokens.shape[1]
    units = down_weight.shape[0]
    hidden_units = units * seqs
    local_count = tokens.shape[0]
    length = local_count * ranks
    width = H * HD // ranks

    def row_factor(values):
        return lax.rsqrt(jnp.mean(values * values, axis=-1, keepdims=True) + EPSILON)

    inputs = tokens.astype(f32)
    factor_one = row_factor(inputs)
    own_gains = jnp.concatenate([attention_gain, feedforward_gain]).astype(f32)[None]
    spread, last = double_to(own_gains, seqs)
    tokens_first = gather_first(tokens)

    def split_heads(weight):
        return jnp.repeat(weight.reshape(rows, KV, HD), ranks // KV, axis=1)

    mix = jnp.concatenate(
        [
            query_weight.reshape(rows, ranks, width),
            split_heads(key_weight),
            split_heads(value_weight),
        ],
        axis=2,
    ).transpose(1, 0, 2)
    gain_one_row, gain_two_row, seg_row, small = gather_small(spread, segments)
    mix = exchange_ctx(after(mix, last)).reshape(ranks * rows, -1)
    mix_wide = gather_seq(mix)
    gain_one_row, gain_two_row, seg_row, small = gather_small(spread, segments)
    tokens_second = gather_second(lax.optimization_barrier((tokens_first, mix))[0])
    pair = split_units(after(gate_weight, mix, *small), up_weight, units)
    pair = exchange_ctx(pair).reshape(ranks * rows, -1)
    proj = lax.ppermute(after(projection, mix), BOTH, head_order())
    proj_wide = gather_seq(proj)

    start = jnp.sum((seg_row < seg_row.T).astype(jnp.int32), axis=1)
    positions = jnp.arange(length, dtype=jnp.int32) - start
    freqs = jnp.power(10000.0, -jnp.arange(HALF, dtype=f32) * (2.0 / HD))
    angles = freqs[:, None] * positions.astype(f32)[None, :]
    cosine, sine_part = jnp.cos(angles), jnp.sin(angles)
    start_row = start[None, :]

    def normalize(piece, gain):
        piece = piece.astype(f32)
        return (piece * row_factor(piece) * gain).astype(bf16)

    normed_all = gather_place(tokens_second, True, normalize, (gain_one_row,))
    pair = after(pair, normed_all)
    pair_wide = gather_seq(pair)
    mixed = dot(mix_wide, normed_all, ((0,), (1,)))
    query_t = rotate(mixed[:width], cosine, sine_part).astype(bf16) * bf16(HD**-0.5)
    key_t = rotate(mixed[width : width + HD], cosine, sine_part).astype(bf16)
    value_t = mixed[width + HD :].astype(bf16)
    query_t = after(query_t, pair)
    key_n, value_n = key_t.T, value_t.T
    cotangent_pieces = send_chips(after(cotangent, normed_all))
    out_t, out_low, lse = attention_forward(query_t, key_n, value_t, start_row)
    out_low, cotangent_pieces = lax.optimization_barrier((out_low, cotangent_pieces))
    down_wide = gather_seq(after(down_weight, out_low))
    rows_by = ((1,), (0,))
    hidden = inputs + scatter_pairs(pair_up(out_low, proj_wide, rows_by))

    factor_two = row_factor(hidden)
    normed_two = (hidden * factor_two * gain_two_row).astype(bf16)
    cotangent_pieces, normed_two = lax.optimization_barrier((cotangent_pieces, normed_two))
    normed_two_first = gather_first(normed_two)
    cotangent_all = place_chips(cotangent_pieces, natural=False)
    columns_by = ((1,), (1,))
    normed_two_all = gather_place(gather_second(normed_two_first), natural=False)
    activated, slope, swished = by_rows(
        functools.partial(units_kernel, hidden_units),
        [normed_two_all],
        pair_wide,
        [hidden_units] * 3,
        "hidden_layer",
    )

    grad_down = dot(activated, cotangent_all, ((0,), (0,)), bf16)
    back = functools.partial(units_back_kernel, hidden_units)
    given = [after(cotangent_all, grad_down), slope, swished]
    wide = [2 * hidden_units, depth]
    both = (4, pair_wide)
    back_away, away = by_rows(back, given, down_wide, wide, "hidden_back_away", (1, 2), both)
    given[0] = after(given[0], away)
    given.append(swap(away, 1, ranks))
    back_stay, two_pairs = by_rows(back, given, down_wide, wide, "hidden_back_stay", (0, 2), both)
    two_pairs = blocks_of(two_pairs)
    grad_down = scatter_seq(grad_down).astype(f32)
    two_first, back_stay = scatter_first(two_pairs, back_stay)
    shaped_two, _ = scatter_rest(two_first)
    shaped_two = shaped_two * gain_two_row
    grad_pair = outer(normed_two_all, [back_stay, back_away])
    shaped_two = after(shaped_two, grad_pair)
    grad_pair = scatter_seq(grad_pair)
    mean_two = jnp.mean(shaped_two * hidden, axis=-1, keepdims=True)
    grad_hidden = (
        cotangent.astype(f32)
        + factor_two * shaped_two
        - hidden * (factor_two * factor_two * factor_two * mean_two)
    )

    branch_first, activated = gather_first(grad_hidden.astype(bf16), activated)
    branch_second = gather_second(branch_first)
    away = product([activated], down_wide, rows_by, (1, 2), "out_away")
    given = [after(activated, away), swap(away, 1, ranks)]
    out_pairs = blocks_of(product(given, down_wide, rows_by, (0, 2), "out_stay"))
    branch_second, out_pairs = lax.optimization_barrier((branch_second, out_pairs))
    out_first, _ = scatter_first(out_pairs)
    branch_all = gather_place(branch_second)
    grad_proj = dot(out_low, branch_all, ((0,), (0,)), bf16)
    grad_out_t = after(dot(proj_wide, branch_all, columns_by, bf16), grad_proj, grad_pair)
    grad_out_t, out_first = lax.optimization_barrier((grad_out_t, out_first))
    out_sum, out_last = scatter_rest(out_first)
    grad_proj, came = to_owners(grad_proj)
    grad_out_t = after(grad_out_t, *came)
    grad_proj = scatter_seq(grad_proj)
    grad_query_t, grad_key_t, grad_value_t = attention_backward(
        query_t, key_n, key_t, value_n, grad_out_t, out_t, lse, start_row
    )
    grad_mixed = jnp.concatenate(
        [
            rotate(grad_query_t * HD**-0.5, cosine, -sine_part),
            rotate(grad_key_t, cosine, -sine_part),
            grad_value_t,
        ],
        axis=0,
    ).astype(bf16)
    grad_pair = exchange_ctx(grad_pair.reshape(ranks, rows, -1))
    grad_mixed = after(grad_mixed, grad_down, grad_pair, grad_proj)
    grad_mix = dot(normed_all, grad_mixed, ((0,), (1,)), bf16)
    block_out = (hidden + out_sum).astype(bf16)
    mixed_n = after(grad_mixed.T, grad_mix, *out_last)
    grad_mix = scatter_seq(grad_mix)
    shaped_one = pair_up(mixed_n, mix_wide, columns_by)
    grad_gate, grad_up, grad_feedforward = join_units(grad_pair, gate_weight, up_weight, units)
    shaped_first, _ = scatter_first(shaped_one)
    shaped_first, grad_mix = lax.optimization_barrier((shaped_first, grad_mix, grad_gate))[:2]
    shaped_one, arrived = scatter_rest(shaped_first)
    shaped_one = shaped_one * gain_one_row
    mean_one = jnp.mean(shaped_one * inputs, axis=-1, keepdims=True)
    grad_tokens = (
        grad_hidden
        + factor_one * shaped_one
        - inputs * (factor_one * factor_one * factor_one * mean_one)
    )

    def join_heads(part):
        part = part.reshape(KV, ranks // KV, rows, HD).astype(f32).sum(axis=1)
        return part.transpose(1, 0, 2).reshape(rows, -1)

    def row_sum(grad, weight):
        return jnp.sum(grad * weight.astype(f32), axis=1)

    grad_feedforward = grad_feedforward[:, 0] / feedforward_gain.astype(f32)

    grad_mix = exchange_ctx(grad_mix.reshape(ranks, rows, -1))
    grad_query = grad_mix[:, :, :width].transpose(1, 0, 2).reshape(rows, -1).astype(f32)
    grad_key = join_heads(grad_mix[:, :, width : width + HD])
    grad_value = join_heads(grad_mix[:, :, width + HD :])
    grad_attention = (
        row_sum(grad_query, query_weight)
        + row_sum(grad_key, key_weight)
        + row_sum(grad_value, value_weight)
    ) / attention_gain.astype(f32)
    grad_projection = grad_proj.astype(f32)
    return (
        block_out,
        grad_tokens,
        grad_attention,
        grad_query,
        grad_key,
        grad_value,
        grad_projection,
        grad_feedforward,
        grad_gate,
        grad_up,
        grad_down,
    )


def solution(mesh):
    rows, plain = P(BOTH, None), P(BOTH)
    return jax.shard_map(
        body,
        mesh=mesh,
        in_specs=(rows, P("seq", "ctx"), rows, plain, rows, rows, rows, rows, plain, rows, rows, rows),
        out_specs=(rows, rows, plain, rows, rows, rows, rows, plain, rows, rows, rows),
        check_vma=False,
    )
```

```python
import functools

import jax
import jax.numpy as jnp
from jax import lax
from jax.experimental import pallas as pl
from jax.experimental.pallas import tpu as pltpu
from jax.sharding import PartitionSpec as P

H = 32
KV = 4
HD = 64
HALF = HD // 2

EPSILON = 1e-05
MASKED = -1e30
BOTH = ("seq", "ctx")
f32 = jnp.float32
bf16 = jnp.bfloat16
LIGHT = pl.CostEstimate(flops=0, transcendentals=0, bytes_accessed=0)


def dot(left, right, contract, out=f32):
    return lax.dot_general(left, right, (contract, ((), ())), preferred_element_type=f32).astype(out)


def after(value, *others):
    return lax.optimization_barrier((value, *others))[0]


def swap(value, step, count):
    return lax.ppermute(value, "ctx", [(i, i ^ step) for i in range(count)])


def blank(shape, dtype):
    return pl.pallas_call(
        lambda out_ref: None,
        out_shape=jax.ShapeDtypeStruct(shape, dtype),
        out_specs=pl.BlockSpec(memory_space=pl.ANY),
        name="blank",
    )()


def chip_bits():
    me = lax.axis_index("ctx")
    count = lax.axis_size("ctx")
    bits = [1 << at for at in range(1, count.bit_length() - 1)]
    return [(step, (me // step) % 2) for step in bits]


def gather_first(value, beside=None):
    count = lax.axis_size("ctx")
    bits = chip_bits()
    half = value.shape[0] // 2
    steps = (bits[0][0], bits[-1][0])
    parts = [value[:half], value[half:]]
    if beside is not None:
        parts, beside = lax.optimization_barrier((parts, beside))
    first = [(part, swap(part, step, count)) for part, step in zip(parts, steps)]
    return first if beside is None else (first, beside)


def gather_second(first):
    count = lax.axis_size("ctx")
    bits = chip_bits()
    parts = []
    for which, (current, arrived) in enumerate(first):
        half, depth = current.shape
        order = list(range(len(bits)))
        if which:
            order.reverse()
        current = current.reshape((1,) * len(bits) + (half, depth))
        arrived = arrived.reshape(current.shape)
        for at in order:
            step, bit = bits[at]
            axis = len(bits) - 1 - at
            if at != order[0]:
                arrived = swap(current, step, count)
            if at != order[-1]:
                current = jnp.where(
                    bit == 0,
                    jnp.concatenate([current, arrived], axis),
                    jnp.concatenate([arrived, current], axis),
                )
        parts.append((current, arrived))
    return parts


def place_kernel(bits, steps, natural, change, *refs):
    parts = 4 * 2
    given, gains = refs[:parts], refs[parts:-4]
    whole, held, ready, done = refs[-4:]
    me = lax.axis_index("ctx")
    core = lax.rem(me, 2)
    arrivals = [pltpu.make_async_copy(ref, held.at[i], ready.at[i]) for i, ref in enumerate(given)]
    copies = []
    for arrival in arrivals:
        arrival.start()
    for number, arrival in enumerate(arrivals):
        which, late, there = number // 4, number // 2 % 2, number % 2
        at = 0 if which else bits - 1
        axis = bits - 1 - at
        index = lax.rem(me // steps[at], 2)
        index = 1 - index if late else index
        owner = 1 - core if there else core
        spot = [slice(None)] * bits
        spot[axis] = index
        arrival.wait()
        if change is not None:
            held[number] = change(held[number], *[ref[...] for ref in gains])
        place = (*spot, owner, which) if natural else (there, *spot, which)
        copy = pltpu.make_async_copy(held.at[number], whole.at[place], done.at[number])
        copy.start()
        copies.append(copy)
    for copy in copies:
        copy.wait()


def gather_place(parts, natural=True, change=None, gains=()):
    count = lax.axis_size("ctx")
    steps = tuple(step for step, _ in chip_bits())
    half, depth = parts[0][0].shape[-2:]
    pieces = []
    for pair in parts:
        for part in pair:
            pieces += [part, swap(part, 1, count)]
    pieces = [piece.reshape((2,) * (len(steps) - 1) + (half, depth)) for piece in pieces]
    anywhere = pl.BlockSpec(memory_space=pl.ANY)
    dtype = pieces[0].dtype
    whole = pl.pallas_call(
        functools.partial(place_kernel, len(steps), steps, natural, change),
        in_specs=[anywhere] * len(pieces) + [pl.BlockSpec(memory_space=pltpu.VMEM)] * len(gains),
        out_specs=anywhere,
        out_shape=jax.ShapeDtypeStruct((2,) * len(steps) + (2, 2, half, depth), dtype),
        scratch_shapes=[
            pltpu.VMEM((len(pieces),) + pieces[0].shape, dtype),
            pltpu.SemaphoreType.DMA((len(pieces),)),
            pltpu.SemaphoreType.DMA((len(pieces),)),
        ],
        compiler_params=pltpu.CompilerParams(vmem_limit_bytes=48 * 1024 * 1024),
        cost_estimate=LIGHT,
        name="place",
    )(*pieces, *gains)
    return whole.reshape(2 * count * half, depth)


def send_chips(value):
    count = lax.axis_size("ctx")
    return {step: swap(value, step, count) if step else value for step in range(0, count, 2)}


def place_chips(pieces, natural=True):
    count = lax.axis_size("ctx")
    me = lax.axis_index("ctx")
    whole = blank((count,) + pieces[0].shape, pieces[0].dtype)
    for step, piece in pieces.items():
        for there in range(2):
            spot = me ^ step ^ there if natural else there * (count // 2) + (me ^ step) // 2
            piece = swap(piece, 1, count) if there else piece
            whole = lax.dynamic_update_index_in_dim(whole, piece, spot, 0)
    return whole.reshape((-1,) + pieces[0].shape[1:])


def double(value, step):
    seqs = lax.axis_size("seq")
    bit = (lax.axis_index("seq") // step) % 2
    other = lax.ppermute(value, "seq", [(i, i ^ step) for i in range(seqs)])
    whole = jnp.where(bit == 0, jnp.concatenate([value, other]), jnp.concatenate([other, value]))
    return whole, other


def double_to(value, end):
    step, other = 1, value
    while step < end:
        value, other = double(value, step)
        step *= 2
    return value, other


def head_order():
    seqs, ranks = lax.axis_size("seq"), lax.axis_size("ctx")
    return [(i, (i % seqs) * ranks + i // seqs) for i in range(seqs * ranks)]


def to_owners(value):
    seqs, ranks = lax.axis_size("seq"), lax.axis_size("ctx")
    me = lax.axis_index("ctx")
    share = ranks // seqs
    blocks = value.reshape(seqs, -1, value.shape[1])
    whole = blank(blocks.shape, value.dtype)
    came = []
    for turn in range(seqs):
        piece = lax.dynamic_index_in_dim(blocks, (me // share + seqs - turn) % seqs, 0, False)
        pairs = [(r, r % share * seqs + (r // share - turn) % seqs) for r in range(ranks)]
        came.append(lax.ppermute(piece, "ctx", pairs))
        spot = (me % seqs + turn) % seqs
        whole = lax.dynamic_update_index_in_dim(whole, came[-1], spot, 0)
    return whole.reshape(value.shape), came


def of_core(value, core):
    count = lax.axis_size("ctx")
    blocks = value.reshape(count // 2, 2, value.shape[0] // count, value.shape[1])
    return lax.dynamic_index_in_dim(blocks, core, 1, keepdims=False).reshape(-1, value.shape[1])


def blocks_of(pairs):
    return pairs.reshape(lax.axis_size("ctx") // 2, -1, pairs.shape[1])


def pair_up(left, right, contract):
    core = lax.axis_index("ctx") % 2
    away = dot(of_core(left, 1 - core), right, contract, bf16)
    arrived = swap(away, 1, lax.axis_size("ctx"))
    stay = after(of_core(left, core), away)
    return blocks_of((dot(stay, right, contract) + arrived.astype(f32)).astype(bf16))


def scatter_parts(current, at):
    bit = chip_bits()[at][1]
    axis = current.ndim - 3 - at
    stay = lax.dynamic_slice_in_dim(current, bit, 1, axis).astype(f32)
    return stay, lax.dynamic_slice_in_dim(current, 1 - bit, 1, axis).astype(bf16)


def scatter_first(pairs, beside=()):
    count = lax.axis_size("ctx")
    bits = chip_bits()
    half, depth = pairs.shape[1] // 2, pairs.shape[2]
    pairs = pairs.reshape((2,) * len(bits) + (2, half, depth))
    low = scatter_parts(pairs[..., 0, :, :], 0)
    high = scatter_parts(pairs[..., 1, :, :], len(bits) - 1)
    aways, beside = lax.optimization_barrier(((low[1], high[1]), beside))
    first = [
        (stay, swap(away, bits[at][0], count))
        for (stay, _), away, at in ((low, aways[0], 0), (high, aways[1], len(bits) - 1))
    ]
    return first, beside


def scatter_rest(first):
    count = lax.axis_size("ctx")
    bits = chip_bits()
    last = []
    sums = []
    for which, (stay, arrived) in enumerate(first):
        for at in range(1, len(bits)):
            at = len(bits) - 1 - at if which else at
            stay, away = scatter_parts(stay + arrived.astype(f32), at)
            arrived = swap(away, bits[at][0], count)
        last.append(arrived)
        sums.append(stay + arrived.astype(f32))
    return jnp.concatenate([part.reshape(part.shape[-2:]) for part in sums]), last


def scatter_pairs(pairs):
    return scatter_rest(scatter_first(pairs)[0])[0]


def gather_seq(value):
    return lax.all_gather(value, "seq", axis=0, tiled=True)


def scatter_seq(value):
    return lax.psum_scatter(value, "seq", scatter_dimension=0, tiled=True)


def exchange_ctx(value):
    return lax.all_to_all(value, "ctx", 0, 0)


def small_rows(spread, segments, width):
    line = jnp.concatenate([spread.reshape(-1), segments.reshape(-1).astype(f32)]).astype(bf16)
    count = -(-line.size // (16 * width)) * 16
    return jnp.pad(line, (0, count * width - line.size)).reshape(count, width)


def read_small(table, spread, segments):
    ranks, seqs = table.shape[0], spread.shape[0]
    table = table.reshape(ranks, -1)
    width, count = spread.size, segments.size
    gains = table[:, :width].reshape(ranks, seqs, 2, -1).transpose(2, 1, 0, 3).reshape(2, -1)
    gains = gains.astype(f32)
    return gains[:1], gains[1:], table[:, width : width + count].astype(f32).reshape(1, -1)


def unit_pieces(seqs, ranks, units):
    wide = seqs * units
    main = wide // 128 * 128
    for rank in range(ranks):
        for which in range(2):
            for seq in range(seqs):
                first, at, end = (seq * ranks + rank) * units, seq * units, (seq + 1) * units
                if at < main:
                    yield rank, which, first, which * main + at, min(end, main) - at
                if end > main:
                    cut = max(at, main)
                    to = 2 * main + which * (wide - main) + cut - main
                    yield rank, which, first + cut - at, to, end - cut


def split_kernel(pieces, gate_ref, up_ref, out_ref):
    refs = (gate_ref, up_ref)
    for rank, which, first, to, size in pieces:
        out_ref[rank, :, to : to + size] = refs[which][:, first : first + size]


def split_units(gate, up, units):
    seqs, ranks = lax.axis_size("seq"), lax.axis_size("ctx")
    return pl.pallas_call(
        functools.partial(split_kernel, tuple(unit_pieces(seqs, ranks, units))),
        out_shape=jax.ShapeDtypeStruct((ranks, gate.shape[0], 2 * seqs * units), gate.dtype),
        compiler_params=pltpu.CompilerParams(vmem_limit_bytes=48 * 1024 * 1024),
        name="split_units",
    )(gate, up)


def join_kernel(pieces, grad_ref, gate_ref, up_ref, grad_gate_ref, grad_up_ref, sum_ref):
    refs = (grad_gate_ref, grad_up_ref)
    for rank, which, first, to, size in pieces:
        refs[which][:, first : first + size] = grad_ref[rank, :, to : to + size].astype(f32)
    terms = grad_gate_ref[...] * gate_ref[...].astype(f32)
    terms = terms + grad_up_ref[...] * up_ref[...].astype(f32)
    sum_ref[...] = jnp.sum(terms, axis=1, keepdims=True)


def join_units(grad, gate, up, units):
    seqs, ranks = lax.axis_size("seq"), lax.axis_size("ctx")
    whole = jax.ShapeDtypeStruct(gate.shape, f32)
    return pl.pallas_call(
        functools.partial(join_kernel, tuple(unit_pieces(seqs, ranks, units))),
        out_shape=[whole, whole, jax.ShapeDtypeStruct((gate.shape[0], 1), f32)],
        compiler_params=pltpu.CompilerParams(vmem_limit_bytes=48 * 1024 * 1024),
        name="join_units",
    )(grad, gate, up)


def spans_of(hidden):
    main = hidden // 128 * 128
    return [(0, main)] + ([(main, hidden - main)] if main < hidden else [])


def units_kernel(hidden, row_ref, weight_ref, out_ref, slope_ref, swished_ref):
    both = dot(row_ref[...], weight_ref[...], ((1,), (0,)))
    for first, size in spans_of(hidden):
        span = slice(first, first + size)
        gate = both[:, 2 * first : 2 * first + size]
        upward = both[:, 2 * first + size : 2 * first + 2 * size]
        sigmoid_gate = jax.nn.sigmoid(gate)
        swished = gate * sigmoid_gate
        out_ref[:, span] = (swished * upward).astype(bf16)
        slope_ref[:, span] = (upward * sigmoid_gate * (1.0 + gate * (1.0 - sigmoid_gate))).astype(bf16)
        swished_ref[:, span] = swished.astype(bf16)


def units_back_kernel(hidden, grad_ref, down_ref, slope_ref, swished_ref, weight_ref, *refs):
    *given, out_ref, product_ref = refs
    grads = dot(grad_ref[...], down_ref[...], ((1,), (1,)))
    for first, size in spans_of(hidden):
        span = slice(first, first + size)
        grad = grads[:, span]
        out_ref[:, 2 * first : 2 * first + size] = (grad * slope_ref[:, span].astype(f32)).astype(bf16)
        out_ref[:, 2 * first + size : 2 * first + 2 * size] = (
            grad * swished_ref[:, span].astype(f32)
        ).astype(bf16)
    product = dot(out_ref[...], weight_ref[...], ((1,), (1,)))
    for ref in given:
        product = product + ref[...].astype(f32)
    product_ref[...] = product.astype(bf16)


def product_kernel(contract, row_ref, weight_ref, *refs):
    out = dot(row_ref[...], weight_ref[...], contract)
    for ref in refs[:-1]:
        out = out + ref[...].astype(f32)
    refs[-1][...] = out.astype(bf16)


def by_rows(kernel, rows, weight, widths, name, part=None, also=None, cost=LIGHT):
    number, parts = part or (0, 1)
    count = rows[0].shape[0] // parts
    block = 256 if count % 256 == 0 else count

    def spec(array):
        first = number * (count // block) if array.shape[0] != count else 0
        return pl.BlockSpec((block, array.shape[1]), lambda i: (i + first, 0))

    arrays = list(rows)
    specs = [spec(array) for array in rows]
    for place, whole in ((1, weight), also or (0, None)):
        if whole is not None:
            arrays.insert(place, whole)
            specs.insert(place, pl.BlockSpec(whole.shape, lambda i: (0, 0)))
    return pl.pallas_call(
        kernel,
        grid=(count // block,),
        in_specs=specs,
        out_specs=[pl.BlockSpec((block, width), lambda i: (i, 0)) for width in widths],
        out_shape=[jax.ShapeDtypeStruct((count, width), bf16) for width in widths],
        compiler_params=pltpu.CompilerParams(vmem_limit_bytes=56 * 1024 * 1024),
        cost_estimate=cost,
        name=name,
    )(*arrays)


HIDDEN_COST = pl.CostEstimate(flops=7_000_000_000, transcendentals=0, bytes_accessed=0)


def product(rows, weight, contract, part, name, cost=HIDDEN_COST):
    kernel = functools.partial(product_kernel, contract)
    width = weight.shape[1 - contract[1][0]]
    return by_rows(kernel, rows, weight, [width], name, part, None, cost)[0]


def outer_kernel(row_ref, *refs):
    *others, out_ref = refs
    first, total = 0, 0.0
    for ref in others:
        end = first + ref.shape[0]
        total = total + dot(row_ref[first:end, :], ref[...], ((0,), (0,)))
        first = end
    out_ref[...] = total.astype(bf16)


def outer(row, others):
    count, depth = row.shape
    width = others[0].shape[1]
    block = 512 if depth % 512 == 0 else depth
    return pl.pallas_call(
        outer_kernel,
        grid=(depth // block,),
        in_specs=[pl.BlockSpec((count, block), lambda i: (0, i))]
        + [pl.BlockSpec(other.shape, lambda i: (0, 0)) for other in others],
        out_specs=pl.BlockSpec((block, width), lambda i: (i, 0)),
        out_shape=jax.ShapeDtypeStruct((depth, width), bf16),
        compiler_params=pltpu.CompilerParams(vmem_limit_bytes=56 * 1024 * 1024),
        cost_estimate=LIGHT,
        name="outer",
    )(row, *others)


def attention_block(length):
    return 512 if length % 512 == 0 else length


def forward_kernel(
    block, heads, count, key_ref, value_ref, query_ref, start_ref, out_ref, out_n_ref, lse_ref
):
    def queries(at):
        end = (at + 1) * block
        rows = lax.broadcasted_iota(jnp.int32, (end, block), 0)
        columns = lax.broadcasted_iota(jnp.int32, (end, block), 1) + at * block
        allowed = (rows >= start_ref[...]) & (rows <= columns)
        for head in range(heads):
            span = slice(head * HD, (head + 1) * HD)
            scores = dot(key_ref[:end, :], query_ref[span, :], ((1,), (0,)))
            scores = jnp.where(allowed, scores, MASKED)
            top = jnp.max(scores, axis=0, keepdims=True)
            weights = jnp.exp(scores - top)
            mass = jnp.sum(weights, axis=0, keepdims=True)
            out = dot(value_ref[:, :end], weights.astype(bf16), ((1,), (0,))) / mass
            out_ref[span, :] = out
            out_n_ref[:, span] = out.T.astype(bf16)
            lse_ref[head : head + 1, :] = top + jnp.log(mass)

    for at in range(count):
        pl.when(pl.program_id(0) == at)(functools.partial(queries, at))


def attention_forward(query_t, key_n, value_t, start):
    width, length = query_t.shape
    heads = width // HD
    block = attention_block(length)
    return pl.pallas_call(
        functools.partial(forward_kernel, block, heads, length // block),
        grid=(length // block,),
        in_specs=[
            pl.BlockSpec((length, HD), lambda i: (0, 0)),
            pl.BlockSpec((HD, length), lambda i: (0, 0)),
            pl.BlockSpec((width, block), lambda i: (0, i)),
            pl.BlockSpec((1, block), lambda i: (0, i)),
        ],
        out_specs=[
            pl.BlockSpec((width, block), lambda i: (0, i)),
            pl.BlockSpec((block, width), lambda i: (i, 0)),
            pl.BlockSpec((heads, block), lambda i: (0, i)),
        ],
        out_shape=[
            jax.ShapeDtypeStruct((width, length), f32),
            jax.ShapeDtypeStruct((length, width), bf16),
            jax.ShapeDtypeStruct((heads, length), f32),
        ],
        compiler_params=pltpu.CompilerParams(vmem_limit_bytes=56 * 1024 * 1024),
        cost_estimate=LIGHT,
        name="attention_forward",
    )(key_n, value_t, query_t, start)


def backward_kernel(
    block,
    heads,
    count,
    key_ref,
    key_t_ref,
    value_ref,
    query_ref,
    grad_ref,
    out_ref,
    lse_ref,
    start_ref,
    grad_query_ref,
    grad_key_ref,
    grad_value_ref,
    query_n,
    grad_n,
    delta,
):
    spans = [slice(head * HD, (head + 1) * HD) for head in range(heads)]

    @pl.when(pl.program_id(0) == 0)
    def _():
        grad_query_ref[...] = jnp.zeros_like(grad_query_ref)
        for head, span in enumerate(spans):
            grads = grad_ref[span, :].astype(f32)
            query_n[head] = query_ref[span, :].astype(f32).T.astype(bf16)
            grad_n[head] = grads.T.astype(bf16)
            delta[head : head + 1, :] = jnp.sum(grads * out_ref[span, :], axis=0, keepdims=True)

    def keys(at):
        low = at * block
        shape = (block, (count - at) * block)
        rows = lax.broadcasted_iota(jnp.int32, shape, 0) + low
        columns = lax.broadcasted_iota(jnp.int32, shape, 1) + low
        allowed = (rows >= start_ref[:, low:]) & (rows <= columns)
        key_sum = jnp.zeros((block, HD), f32)
        value_sum = jnp.zeros((block, HD), f32)
        for head, span in enumerate(spans):
            scores = dot(key_ref[...], query_ref[span, low:], ((1,), (0,)))
            scores = jnp.where(allowed, scores, MASKED)
            probs = jnp.exp(scores - lse_ref[head : head + 1, low:])
            value_sum += dot(probs.astype(bf16), grad_n[head, low:, :], ((1,), (0,)))
            grad_probs = dot(value_ref[...], grad_ref[span, low:], ((1,), (0,)))
            grad_scores = (probs * (grad_probs - delta[head : head + 1, low:])).astype(bf16)
            key_sum += dot(grad_scores, query_n[head, low:, :], ((1,), (0,)))
            grad_query_ref[span, low:] += dot(key_t_ref[...], grad_scores, ((1,), (0,)))
        grad_key_ref[...] = key_sum.T
        grad_value_ref[...] = value_sum.T

    for at in range(count):
        pl.when(pl.program_id(0) == at)(functools.partial(keys, at))


def attention_backward(query_t, key_n, key_t, value_n, grad_t, out_t, lse, start):
    width, length = query_t.shape
    heads = width // HD
    block = attention_block(length)
    count = length // block

    def whole(j):
        return 0, 0

    return pl.pallas_call(
        functools.partial(backward_kernel, block, heads, count),
        grid=(count,),
        in_specs=[
            pl.BlockSpec((block, HD), lambda j: (j, 0)),
            pl.BlockSpec((HD, block), lambda j: (0, j)),
            pl.BlockSpec((block, HD), lambda j: (j, 0)),
            pl.BlockSpec((width, length), whole),
            pl.BlockSpec((width, length), whole),
            pl.BlockSpec((width, length), whole),
            pl.BlockSpec((heads, length), whole),
            pl.BlockSpec((1, length), whole),
        ],
        out_specs=[
            pl.BlockSpec((width, length), whole),
            pl.BlockSpec((HD, block), lambda j: (0, j)),
            pl.BlockSpec((HD, block), lambda j: (0, j)),
        ],
        out_shape=[
            jax.ShapeDtypeStruct((width, length), f32),
            jax.ShapeDtypeStruct((HD, length), f32),
            jax.ShapeDtypeStruct((HD, length), f32),
        ],
        scratch_shapes=[
            pltpu.VMEM((heads, length, HD), bf16),
            pltpu.VMEM((heads, length, HD), bf16),
            pltpu.VMEM((heads, length), f32),
        ],
        cost_estimate=pl.CostEstimate(flops=25_000_000_000, transcendentals=0, bytes_accessed=0),
        compiler_params=pltpu.CompilerParams(vmem_limit_bytes=56 * 1024 * 1024),
        name="attention_backward",
    )(key_n, key_t, value_n, query_t, grad_t, out_t, lse, start)


def rotate(source, cosine, sine_part):
    halves = source.reshape(-1, 2, HALF, source.shape[1])
    first, second = halves[:, 0], halves[:, 1]
    turned = jnp.stack(
        [first * cosine - second * sine_part, second * cosine + first * sine_part], axis=1
    )
    return turned.reshape(source.shape)


def body(
    tokens,
    segments,
    cotangent,
    attention_gain,
    query_weight,
    key_weight,
    value_weight,
    projection,
    feedforward_gain,
    gate_weight,
    up_weight,
    down_weight,
):
    seqs, ranks = lax.axis_size("seq"), lax.axis_size("ctx")
    rows = query_weight.shape[0]
    depth = tokens.shape[1]
    units = down_weight.shape[0]
    hidden_units = units * seqs
    local_count = tokens.shape[0]
    length = local_count * ranks
    width = H * HD // ranks

    def row_factor(values):
        return lax.rsqrt(jnp.mean(values * values, axis=-1, keepdims=True) + EPSILON)

    inputs = tokens.astype(f32)
    factor_one = row_factor(inputs)
    own_gains = jnp.concatenate([attention_gain, feedforward_gain]).astype(f32)[None]
    spread, last = double_to(own_gains, seqs)
    tokens_first = gather_first(tokens)

    def split_heads(weight):
        return jnp.repeat(weight.reshape(rows, KV, HD), ranks // KV, axis=1)

    mix = jnp.concatenate(
        [
            query_weight.reshape(rows, ranks, width),
            split_heads(key_weight),
            split_heads(value_weight),
        ],
        axis=2,
    ).transpose(1, 0, 2)
    small = small_rows(spread, segments, mix.shape[2])
    small = jnp.broadcast_to(small[None], (ranks,) + small.shape)
    mix = exchange_ctx(jnp.concatenate([mix, small], axis=1))
    gain_one_row, gain_two_row, seg_row = read_small(mix[:, rows:], spread, segments)
    mix = mix[:, :rows].reshape(ranks * rows, -1)
    proj_wide = gather_seq(lax.ppermute(after(projection, last), BOTH, head_order()))
    mix_wide = gather_seq(after(mix, proj_wide))
    tokens_second = gather_second(lax.optimization_barrier((tokens_first, mix))[0])
    pair = split_units(after(gate_weight, mix), up_weight, units)
    pair = exchange_ctx(pair).reshape(ranks * rows, -1)

    start = jnp.sum((seg_row < seg_row.T).astype(jnp.int32), axis=1)
    positions = jnp.arange(length, dtype=jnp.int32) - start
    freqs = jnp.power(10000.0, -jnp.arange(HALF, dtype=f32) * (2.0 / HD))
    angles = freqs[:, None] * positions.astype(f32)[None, :]
    cosine, sine_part = jnp.cos(angles), jnp.sin(angles)
    start_row = start[None, :]

    def normalize(piece, gain):
        piece = piece.astype(f32)
        return (piece * row_factor(piece) * gain).astype(bf16)

    normed_all = gather_place(tokens_second, True, normalize, (gain_one_row,))
    pair = after(pair, normed_all)
    pair_wide = gather_seq(pair)
    mixed = dot(mix_wide, normed_all, ((0,), (1,)))
    query_t = rotate(mixed[:width], cosine, sine_part).astype(bf16) * bf16(HD**-0.5)
    key_t = rotate(mixed[width : width + HD], cosine, sine_part).astype(bf16)
    value_t = mixed[width + HD :].astype(bf16)
    query_t = after(query_t, pair)
    key_n, value_n = key_t.T, value_t.T
    cotangent_pieces = send_chips(after(cotangent, normed_all))
    out_t, out_low, lse = attention_forward(query_t, key_n, value_t, start_row)
    out_low, cotangent_pieces = lax.optimization_barrier((out_low, cotangent_pieces))
    down_wide = gather_seq(after(down_weight, out_low))
    rows_by = ((1,), (0,))
    hidden = inputs + scatter_pairs(pair_up(out_low, proj_wide, rows_by))

    factor_two = row_factor(hidden)
    normed_two = (hidden * factor_two * gain_two_row).astype(bf16)
    cotangent_pieces, normed_two = lax.optimization_barrier((cotangent_pieces, normed_two))
    normed_two_first = gather_first(normed_two)
    cotangent_all = place_chips(cotangent_pieces, natural=False)
    columns_by = ((1,), (1,))
    normed_two_all = gather_place(gather_second(normed_two_first), natural=False)
    activated, slope, swished = by_rows(
        functools.partial(units_kernel, hidden_units),
        [normed_two_all],
        pair_wide,
        [hidden_units] * 3,
        "hidden_layer",
    )

    grad_down = dot(activated, cotangent_all, ((0,), (0,)), bf16)
    back = functools.partial(units_back_kernel, hidden_units)
    given = [after(cotangent_all, grad_down), slope, swished]
    wide = [2 * hidden_units, depth]
    both = (4, pair_wide)
    back_away, away = by_rows(back, given, down_wide, wide, "hidden_back_away", (1, 2), both)
    given[0] = after(given[0], away)
    given.append(swap(away, 1, ranks))
    back_stay, two_pairs = by_rows(back, given, down_wide, wide, "hidden_back_stay", (0, 2), both)
    two_pairs = blocks_of(two_pairs)
    grad_down = scatter_seq(grad_down).astype(f32)
    two_first, back_stay = scatter_first(two_pairs, back_stay)
    shaped_two, _ = scatter_rest(two_first)
    shaped_two = shaped_two * gain_two_row
    grad_pair = outer(normed_two_all, [back_stay, back_away])
    shaped_two = after(shaped_two, grad_pair)
    grad_pair = scatter_seq(grad_pair)
    mean_two = jnp.mean(shaped_two * hidden, axis=-1, keepdims=True)
    grad_hidden = (
        cotangent.astype(f32)
        + factor_two * shaped_two
        - hidden * (factor_two * factor_two * factor_two * mean_two)
    )

    branch_first, activated = gather_first(grad_hidden.astype(bf16), activated)
    branch_second = gather_second(branch_first)
    away = product([activated], down_wide, rows_by, (1, 2), "out_away")
    given = [after(activated, away), swap(away, 1, ranks)]
    out_pairs = blocks_of(product(given, down_wide, rows_by, (0, 2), "out_stay"))
    branch_second, out_pairs = lax.optimization_barrier((branch_second, out_pairs))
    out_first, _ = scatter_first(out_pairs)
    branch_all = gather_place(branch_second)
    grad_proj = dot(out_low, branch_all, ((0,), (0,)), bf16)
    grad_out_t = after(dot(proj_wide, branch_all, columns_by, bf16), grad_proj)
    grad_out_t, out_first = lax.optimization_barrier((grad_out_t, out_first))
    out_sum, out_last = scatter_rest(out_first)
    grad_out_t = after(grad_out_t, *out_last)
    grad_out_t = after(grad_out_t, grad_pair)
    grad_proj, came = to_owners(grad_proj)
    grad_out_t = after(grad_out_t, *came)
    grad_proj = scatter_seq(grad_proj)
    grad_query_t, grad_key_t, grad_value_t = attention_backward(
        query_t, key_n, key_t, value_n, grad_out_t, out_t, lse, start_row
    )
    grad_mixed = jnp.concatenate(
        [
            rotate(grad_query_t * HD**-0.5, cosine, -sine_part),
            rotate(grad_key_t, cosine, -sine_part),
            grad_value_t,
        ],
        axis=0,
    ).astype(bf16)
    grad_pair = exchange_ctx(grad_pair.reshape(ranks, rows, -1))
    grad_mixed = after(grad_mixed, grad_down, grad_pair, grad_proj)
    block_out = (hidden + out_sum).astype(bf16)
    mixed_n = grad_mixed.T
    core = lax.axis_index("ctx") % 2
    parts = [of_core(mixed_n, 1 - core), of_core(mixed_n, core)]
    away = product(parts[:1], mix_wide, columns_by, None, "mixed_away", LIGHT)
    grad_mix = dot(normed_all, after(grad_mixed, away), ((0,), (1,)), bf16)
    grad_mix = scatter_seq(grad_mix)
    parts = [after(parts[1], away), swap(away, 1, ranks)]
    shaped_one = blocks_of(product(parts, mix_wide, columns_by, None, "mixed_stay", LIGHT))
    grad_gate, grad_up, grad_feedforward = join_units(grad_pair, gate_weight, up_weight, units)
    shaped_first, _ = scatter_first(shaped_one)
    shaped_first, grad_mix = lax.optimization_barrier(
        (shaped_first, grad_mix, grad_gate)
    )[:2]
    shaped_one, arrived = scatter_rest(shaped_first)
    shaped_one = shaped_one * gain_one_row
    mean_one = jnp.mean(shaped_one * inputs, axis=-1, keepdims=True)
    grad_tokens = (
        grad_hidden
        + factor_one * shaped_one
        - inputs * (factor_one * factor_one * factor_one * mean_one)
    )

    def join_heads(part):
        part = part.reshape(KV, ranks // KV, rows, HD).astype(f32).sum(axis=1)
        return part.transpose(1, 0, 2).reshape(rows, -1)

    def row_sum(grad, weight):
        return jnp.sum(grad * weight.astype(f32), axis=1)

    grad_feedforward = grad_feedforward[:, 0] / feedforward_gain.astype(f32)

    grad_mix = exchange_ctx(grad_mix.reshape(ranks, rows, -1))
    grad_query = grad_mix[:, :, :width].transpose(1, 0, 2).reshape(rows, -1).astype(f32)
    grad_key = join_heads(grad_mix[:, :, width : width + HD])
    grad_value = join_heads(grad_mix[:, :, width + HD :])
    grad_attention = (
        row_sum(grad_query, query_weight)
        + row_sum(grad_key, key_weight)
        + row_sum(grad_value, value_weight)
    ) / attention_gain.astype(f32)
    grad_projection = grad_proj.astype(f32)
    return (
        block_out,
        grad_tokens,
        grad_attention,
        grad_query,
        grad_key,
        grad_value,
        grad_projection,
        grad_feedforward,
        grad_gate,
        grad_up,
        grad_down,
    )


def solution(mesh):
    rows, plain = P(BOTH, None), P(BOTH)
    return jax.shard_map(
        body,
        mesh=mesh,
        in_specs=(rows, P("seq", "ctx"), rows, plain, rows, rows, rows, rows, plain, rows, rows, rows),
        out_specs=(rows, rows, plain, rows, rows, rows, rows, plain, rows, rows, rows),
        check_vma=False,
    )
```

```python
import functools

import jax
import jax.numpy as jnp
from jax import lax
from jax.experimental import pallas as pl
from jax.experimental.pallas import tpu as pltpu
from jax.sharding import PartitionSpec as P

H = 32
KV = 4
HD = 64
HALF = HD // 2

EPSILON = 1e-05
MASKED = -1e30
BOTH = ("seq", "ctx")
f32 = jnp.float32
bf16 = jnp.bfloat16
LIGHT = pl.CostEstimate(flops=0, transcendentals=0, bytes_accessed=0)


def dot(left, right, contract, out=f32):
    return lax.dot_general(left, right, (contract, ((), ())), preferred_element_type=f32).astype(out)


def after(value, *others):
    return lax.optimization_barrier((value, *others))[0]


def swap(value, step, count):
    return lax.ppermute(value, "ctx", [(i, i ^ step) for i in range(count)])


def blank(shape, dtype):
    return pl.pallas_call(
        lambda out_ref: None,
        out_shape=jax.ShapeDtypeStruct(shape, dtype),
        out_specs=pl.BlockSpec(memory_space=pl.ANY),
        name="blank",
    )()


def chip_bits():
    me = lax.axis_index("ctx")
    count = lax.axis_size("ctx")
    bits = [1 << at for at in range(1, count.bit_length() - 1)]
    return [(step, (me // step) % 2) for step in bits]


def gather_first(value, beside=None):
    count = lax.axis_size("ctx")
    bits = chip_bits()
    half = value.shape[0] // 2
    steps = (bits[0][0], bits[-1][0])
    parts = [value[:half], value[half:]]
    if beside is not None:
        parts, beside = lax.optimization_barrier((parts, beside))
    first = [(part, swap(part, step, count)) for part, step in zip(parts, steps)]
    return first if beside is None else (first, beside)


def gather_second(first):
    count = lax.axis_size("ctx")
    bits = chip_bits()
    parts = []
    for which, (current, arrived) in enumerate(first):
        half, depth = current.shape
        order = list(range(len(bits)))
        if which:
            order.reverse()
        current = current.reshape((1,) * len(bits) + (half, depth))
        arrived = arrived.reshape(current.shape)
        for at in order:
            step, bit = bits[at]
            axis = len(bits) - 1 - at
            if at != order[0]:
                arrived = swap(current, step, count)
            if at != order[-1]:
                current = jnp.where(
                    bit == 0,
                    jnp.concatenate([current, arrived], axis),
                    jnp.concatenate([arrived, current], axis),
                )
        parts.append((current, arrived))
    return parts


def place_kernel(bits, steps, natural, change, *refs):
    parts = 4 * 2
    given, gains = refs[:parts], refs[parts:-4]
    whole, held, ready, done = refs[-4:]
    me = lax.axis_index("ctx")
    core = lax.rem(me, 2)
    arrivals = [pltpu.make_async_copy(ref, held.at[i], ready.at[i]) for i, ref in enumerate(given)]
    copies = []
    for arrival in arrivals:
        arrival.start()
    for number, arrival in enumerate(arrivals):
        which, late, there = number // 4, number // 2 % 2, number % 2
        at = 0 if which else bits - 1
        axis = bits - 1 - at
        index = lax.rem(me // steps[at], 2)
        index = 1 - index if late else index
        owner = 1 - core if there else core
        spot = [slice(None)] * bits
        spot[axis] = index
        arrival.wait()
        if change is not None:
            held[number] = change(held[number], *[ref[...] for ref in gains])
        place = (*spot, owner, which) if natural else (there, *spot, which)
        copy = pltpu.make_async_copy(held.at[number], whole.at[place], done.at[number])
        copy.start()
        copies.append(copy)
    for copy in copies:
        copy.wait()


def gather_place(parts, natural=True, change=None, gains=()):
    count = lax.axis_size("ctx")
    steps = tuple(step for step, _ in chip_bits())
    half, depth = parts[0][0].shape[-2:]
    pieces = []
    for pair in parts:
        for part in pair:
            pieces += [part, swap(part, 1, count)]
    pieces = [piece.reshape((2,) * (len(steps) - 1) + (half, depth)) for piece in pieces]
    anywhere = pl.BlockSpec(memory_space=pl.ANY)
    dtype = pieces[0].dtype
    whole = pl.pallas_call(
        functools.partial(place_kernel, len(steps), steps, natural, change),
        in_specs=[anywhere] * len(pieces) + [pl.BlockSpec(memory_space=pltpu.VMEM)] * len(gains),
        out_specs=anywhere,
        out_shape=jax.ShapeDtypeStruct((2,) * len(steps) + (2, 2, half, depth), dtype),
        scratch_shapes=[
            pltpu.VMEM((len(pieces),) + pieces[0].shape, dtype),
            pltpu.SemaphoreType.DMA((len(pieces),)),
            pltpu.SemaphoreType.DMA((len(pieces),)),
        ],
        compiler_params=pltpu.CompilerParams(vmem_limit_bytes=48 * 1024 * 1024),
        cost_estimate=LIGHT,
        name="place",
    )(*pieces, *gains)
    return whole.reshape(2 * count * half, depth)


def send_chips(value):
    count = lax.axis_size("ctx")
    return {step: swap(value, step, count) if step else value for step in range(0, count, 2)}


def place_chips(pieces, natural=True):
    count = lax.axis_size("ctx")
    me = lax.axis_index("ctx")
    whole = blank((count,) + pieces[0].shape, pieces[0].dtype)
    for step, piece in pieces.items():
        for there in range(2):
            spot = me ^ step ^ there if natural else there * (count // 2) + (me ^ step) // 2
            piece = swap(piece, 1, count) if there else piece
            whole = lax.dynamic_update_index_in_dim(whole, piece, spot, 0)
    return whole.reshape((-1,) + pieces[0].shape[1:])


def double(value, step):
    seqs = lax.axis_size("seq")
    bit = (lax.axis_index("seq") // step) % 2
    other = lax.ppermute(value, "seq", [(i, i ^ step) for i in range(seqs)])
    whole = jnp.where(bit == 0, jnp.concatenate([value, other]), jnp.concatenate([other, value]))
    return whole, other


def double_to(value, end):
    step, other = 1, value
    while step < end:
        value, other = double(value, step)
        step *= 2
    return value, other


def head_order():
    seqs, ranks = lax.axis_size("seq"), lax.axis_size("ctx")
    return [(i, (i % seqs) * ranks + i // seqs) for i in range(seqs * ranks)]


def to_owners(value):
    seqs, ranks = lax.axis_size("seq"), lax.axis_size("ctx")
    me = lax.axis_index("ctx")
    share = ranks // seqs
    blocks = value.reshape(seqs, -1, value.shape[1])
    whole = blank(blocks.shape, value.dtype)
    came = []
    for turn in range(seqs):
        piece = lax.dynamic_index_in_dim(blocks, (me // share + seqs - turn) % seqs, 0, False)
        pairs = [(r, r % share * seqs + (r // share - turn) % seqs) for r in range(ranks)]
        came.append(lax.ppermute(piece, "ctx", pairs))
        spot = (me % seqs + turn) % seqs
        whole = lax.dynamic_update_index_in_dim(whole, came[-1], spot, 0)
    return whole.reshape(value.shape), came


def of_core(value, core):
    count = lax.axis_size("ctx")
    blocks = value.reshape(count // 2, 2, value.shape[0] // count, value.shape[1])
    return lax.dynamic_index_in_dim(blocks, core, 1, keepdims=False).reshape(-1, value.shape[1])


def blocks_of(pairs):
    return pairs.reshape(lax.axis_size("ctx") // 2, -1, pairs.shape[1])


def pair_up(left, right, contract):
    core = lax.axis_index("ctx") % 2
    away = dot(of_core(left, 1 - core), right, contract, bf16)
    arrived = swap(away, 1, lax.axis_size("ctx"))
    stay = after(of_core(left, core), away)
    return blocks_of((dot(stay, right, contract) + arrived.astype(f32)).astype(bf16))


def scatter_parts(current, at):
    bit = chip_bits()[at][1]
    axis = current.ndim - 3 - at
    stay = lax.dynamic_slice_in_dim(current, bit, 1, axis).astype(f32)
    return stay, lax.dynamic_slice_in_dim(current, 1 - bit, 1, axis).astype(bf16)


def scatter_first(pairs, beside=()):
    count = lax.axis_size("ctx")
    bits = chip_bits()
    half, depth = pairs.shape[1] // 2, pairs.shape[2]
    pairs = pairs.reshape((2,) * len(bits) + (2, half, depth))
    low = scatter_parts(pairs[..., 0, :, :], 0)
    high = scatter_parts(pairs[..., 1, :, :], len(bits) - 1)
    aways, beside = lax.optimization_barrier(((low[1], high[1]), beside))
    first = [
        (stay, swap(away, bits[at][0], count))
        for (stay, _), away, at in ((low, aways[0], 0), (high, aways[1], len(bits) - 1))
    ]
    return first, beside


def scatter_rest(first, beside=None):
    count = lax.axis_size("ctx")
    bits = chip_bits()
    kept, last = [], []
    for which, (stay, arrived) in enumerate(first):
        for at in range(1, len(bits)):
            at = len(bits) - 1 - at if which else at
            stay, away = scatter_parts(stay + arrived.astype(f32), at)
            arrived = swap(away, bits[at][0], count)
        kept.append(stay)
        last.append(arrived)
    if beside is not None:
        last, beside = lax.optimization_barrier((last, beside))
    sums = [stay + arrived.astype(f32) for stay, arrived in zip(kept, last)]
    return jnp.concatenate([part.reshape(part.shape[-2:]) for part in sums]), last, beside


def scatter_pairs(pairs):
    return scatter_rest(scatter_first(pairs)[0])[0]


def gather_seq(value):
    return lax.all_gather(value, "seq", axis=0, tiled=True)


def scatter_seq(value):
    return lax.psum_scatter(value, "seq", scatter_dimension=0, tiled=True)


def exchange_ctx(value):
    return lax.all_to_all(value, "ctx", 0, 0)


def small_rows(spread, segments, width):
    line = jnp.concatenate([spread.reshape(-1), segments.reshape(-1).astype(f32)]).astype(bf16)
    count = -(-line.size // (16 * width)) * 16
    return jnp.pad(line, (0, count * width - line.size)).reshape(count, width)


def read_small(table, spread, segments):
    ranks, seqs = table.shape[0], spread.shape[0]
    table = table.reshape(ranks, -1)
    width, count = spread.size, segments.size
    gains = table[:, :width].reshape(ranks, seqs, 2, -1).transpose(2, 1, 0, 3).reshape(2, -1)
    gains = gains.astype(f32)
    return gains[:1], gains[1:], table[:, width : width + count].astype(f32).reshape(1, -1)


def unit_pieces(seqs, ranks, units):
    wide = seqs * units
    main = wide // 128 * 128
    for rank in range(ranks):
        for which in range(2):
            for seq in range(seqs):
                first, at, end = (seq * ranks + rank) * units, seq * units, (seq + 1) * units
                if at < main:
                    yield rank, which, first, which * main + at, min(end, main) - at
                if end > main:
                    cut = max(at, main)
                    to = 2 * main + which * (wide - main) + cut - main
                    yield rank, which, first + cut - at, to, end - cut


def split_kernel(pieces, gate_ref, up_ref, out_ref):
    refs = (gate_ref, up_ref)
    for rank, which, first, to, size in pieces:
        out_ref[rank, :, to : to + size] = refs[which][:, first : first + size]


def split_units(gate, up, units):
    seqs, ranks = lax.axis_size("seq"), lax.axis_size("ctx")
    return pl.pallas_call(
        functools.partial(split_kernel, tuple(unit_pieces(seqs, ranks, units))),
        out_shape=jax.ShapeDtypeStruct((ranks, gate.shape[0], 2 * seqs * units), gate.dtype),
        compiler_params=pltpu.CompilerParams(vmem_limit_bytes=48 * 1024 * 1024),
        name="split_units",
    )(gate, up)


def join_kernel(pieces, grad_ref, gate_ref, up_ref, grad_gate_ref, grad_up_ref, sum_ref):
    refs = (grad_gate_ref, grad_up_ref)
    for rank, which, first, to, size in pieces:
        refs[which][:, first : first + size] = grad_ref[rank, :, to : to + size].astype(f32)
    terms = grad_gate_ref[...] * gate_ref[...].astype(f32)
    terms = terms + grad_up_ref[...] * up_ref[...].astype(f32)
    sum_ref[...] = jnp.sum(terms, axis=1, keepdims=True)


def join_units(grad, gate, up, units):
    seqs, ranks = lax.axis_size("seq"), lax.axis_size("ctx")
    whole = jax.ShapeDtypeStruct(gate.shape, f32)
    return pl.pallas_call(
        functools.partial(join_kernel, tuple(unit_pieces(seqs, ranks, units))),
        out_shape=[whole, whole, jax.ShapeDtypeStruct((gate.shape[0], 1), f32)],
        compiler_params=pltpu.CompilerParams(vmem_limit_bytes=48 * 1024 * 1024),
        name="join_units",
    )(grad, gate, up)


def spans_of(hidden):
    main = hidden // 128 * 128
    return [(0, main)] + ([(main, hidden - main)] if main < hidden else [])


def units_kernel(hidden, row_ref, weight_ref, out_ref, slope_ref, swished_ref):
    both = dot(row_ref[...], weight_ref[...], ((1,), (0,)))
    for first, size in spans_of(hidden):
        span = slice(first, first + size)
        gate = both[:, 2 * first : 2 * first + size]
        upward = both[:, 2 * first + size : 2 * first + 2 * size]
        sigmoid_gate = jax.nn.sigmoid(gate)
        swished = gate * sigmoid_gate
        out_ref[:, span] = (swished * upward).astype(bf16)
        slope_ref[:, span] = (upward * sigmoid_gate * (1.0 + gate * (1.0 - sigmoid_gate))).astype(bf16)
        swished_ref[:, span] = swished.astype(bf16)


def units_back_kernel(hidden, grad_ref, down_ref, slope_ref, swished_ref, weight_ref, *refs):
    *given, out_ref, product_ref = refs
    grads = dot(grad_ref[...], down_ref[...], ((1,), (1,)))
    for first, size in spans_of(hidden):
        span = slice(first, first + size)
        grad = grads[:, span]
        out_ref[:, 2 * first : 2 * first + size] = (grad * slope_ref[:, span].astype(f32)).astype(bf16)
        out_ref[:, 2 * first + size : 2 * first + 2 * size] = (
            grad * swished_ref[:, span].astype(f32)
        ).astype(bf16)
    product = dot(out_ref[...], weight_ref[...], ((1,), (1,)))
    for ref in given:
        product = product + ref[...].astype(f32)
    product_ref[...] = product.astype(bf16)


def product_kernel(contract, row_ref, weight_ref, *refs):
    out = dot(row_ref[...], weight_ref[...], contract)
    for ref in refs[:-1]:
        out = out + ref[...].astype(f32)
    refs[-1][...] = out.astype(bf16)


def by_rows(kernel, rows, weight, widths, name, part=None, also=None, cost=LIGHT):
    number, parts = part or (0, 1)
    count = rows[0].shape[0] // parts
    block = 256 if count % 256 == 0 else count

    def spec(array):
        first = number * (count // block) if array.shape[0] != count else 0
        return pl.BlockSpec((block, array.shape[1]), lambda i: (i + first, 0))

    arrays = list(rows)
    specs = [spec(array) for array in rows]
    for place, whole in ((1, weight), also or (0, None)):
        if whole is not None:
            arrays.insert(place, whole)
            specs.insert(place, pl.BlockSpec(whole.shape, lambda i: (0, 0)))
    return pl.pallas_call(
        kernel,
        grid=(count // block,),
        in_specs=specs,
        out_specs=[pl.BlockSpec((block, width), lambda i: (i, 0)) for width in widths],
        out_shape=[jax.ShapeDtypeStruct((count, width), bf16) for width in widths],
        compiler_params=pltpu.CompilerParams(vmem_limit_bytes=56 * 1024 * 1024),
        cost_estimate=cost,
        name=name,
    )(*arrays)


HIDDEN_COST = pl.CostEstimate(flops=7_000_000_000, transcendentals=0, bytes_accessed=0)


def product(rows, weight, contract, part, name, cost=HIDDEN_COST):
    kernel = functools.partial(product_kernel, contract)
    width = weight.shape[1 - contract[1][0]]
    return by_rows(kernel, rows, weight, [width], name, part, None, cost)[0]


def outer_kernel(row_ref, *refs):
    *others, out_ref = refs
    first, total = 0, 0.0
    for ref in others:
        end = first + ref.shape[0]
        total = total + dot(row_ref[first:end, :], ref[...], ((0,), (0,)))
        first = end
    out_ref[...] = total.astype(bf16)


def outer(row, others):
    count, depth = row.shape
    width = others[0].shape[1]
    block = 512 if depth % 512 == 0 else depth
    return pl.pallas_call(
        outer_kernel,
        grid=(depth // block,),
        in_specs=[pl.BlockSpec((count, block), lambda i: (0, i))]
        + [pl.BlockSpec(other.shape, lambda i: (0, 0)) for other in others],
        out_specs=pl.BlockSpec((block, width), lambda i: (i, 0)),
        out_shape=jax.ShapeDtypeStruct((depth, width), bf16),
        compiler_params=pltpu.CompilerParams(vmem_limit_bytes=56 * 1024 * 1024),
        cost_estimate=LIGHT,
        name="outer",
    )(row, *others)


def attention_block(length):
    return 512 if length % 512 == 0 else length


def forward_kernel(
    block, heads, count, key_ref, value_ref, query_ref, start_ref, out_ref, out_n_ref, lse_ref
):
    def queries(at):
        end = (at + 1) * block
        rows = lax.broadcasted_iota(jnp.int32, (end, block), 0)
        columns = lax.broadcasted_iota(jnp.int32, (end, block), 1) + at * block
        allowed = (rows >= start_ref[...]) & (rows <= columns)
        for head in range(heads):
            span = slice(head * HD, (head + 1) * HD)
            scores = dot(key_ref[:end, :], query_ref[span, :], ((1,), (0,)))
            scores = jnp.where(allowed, scores, MASKED)
            top = jnp.max(scores, axis=0, keepdims=True)
            weights = jnp.exp(scores - top)
            mass = jnp.sum(weights, axis=0, keepdims=True)
            out = dot(value_ref[:, :end], weights.astype(bf16), ((1,), (0,))) / mass
            out_ref[span, :] = out
            out_n_ref[:, span] = out.T.astype(bf16)
            lse_ref[head : head + 1, :] = top + jnp.log(mass)

    for at in range(count):
        pl.when(pl.program_id(0) == at)(functools.partial(queries, at))


def attention_forward(query_t, key_n, value_t, start):
    width, length = query_t.shape
    heads = width // HD
    block = attention_block(length)
    return pl.pallas_call(
        functools.partial(forward_kernel, block, heads, length // block),
        grid=(length // block,),
        in_specs=[
            pl.BlockSpec((length, HD), lambda i: (0, 0)),
            pl.BlockSpec((HD, length), lambda i: (0, 0)),
            pl.BlockSpec((width, block), lambda i: (0, i)),
            pl.BlockSpec((1, block), lambda i: (0, i)),
        ],
        out_specs=[
            pl.BlockSpec((width, block), lambda i: (0, i)),
            pl.BlockSpec((block, width), lambda i: (i, 0)),
            pl.BlockSpec((heads, block), lambda i: (0, i)),
        ],
        out_shape=[
            jax.ShapeDtypeStruct((width, length), f32),
            jax.ShapeDtypeStruct((length, width), bf16),
            jax.ShapeDtypeStruct((heads, length), f32),
        ],
        compiler_params=pltpu.CompilerParams(vmem_limit_bytes=56 * 1024 * 1024),
        cost_estimate=LIGHT,
        name="attention_forward",
    )(key_n, value_t, query_t, start)


def backward_kernel(
    block,
    heads,
    count,
    key_ref,
    key_t_ref,
    value_ref,
    query_ref,
    grad_ref,
    out_ref,
    lse_ref,
    start_ref,
    grad_query_ref,
    grad_key_ref,
    grad_value_ref,
    query_n,
    grad_n,
    delta,
):
    spans = [slice(head * HD, (head + 1) * HD) for head in range(heads)]

    @pl.when(pl.program_id(0) == 0)
    def _():
        grad_query_ref[...] = jnp.zeros_like(grad_query_ref)
        for head, span in enumerate(spans):
            grads = grad_ref[span, :].astype(f32)
            query_n[head] = query_ref[span, :].astype(f32).T.astype(bf16)
            grad_n[head] = grads.T.astype(bf16)
            delta[head : head + 1, :] = jnp.sum(grads * out_ref[span, :], axis=0, keepdims=True)

    def keys(at):
        low = at * block
        shape = (block, (count - at) * block)
        rows = lax.broadcasted_iota(jnp.int32, shape, 0) + low
        columns = lax.broadcasted_iota(jnp.int32, shape, 1) + low
        allowed = (rows >= start_ref[:, low:]) & (rows <= columns)
        key_sum = jnp.zeros((block, HD), f32)
        value_sum = jnp.zeros((block, HD), f32)
        for head, span in enumerate(spans):
            scores = dot(key_ref[...], query_ref[span, low:], ((1,), (0,)))
            scores = jnp.where(allowed, scores, MASKED)
            probs = jnp.exp(scores - lse_ref[head : head + 1, low:])
            value_sum += dot(probs.astype(bf16), grad_n[head, low:, :], ((1,), (0,)))
            grad_probs = dot(value_ref[...], grad_ref[span, low:], ((1,), (0,)))
            grad_scores = (probs * (grad_probs - delta[head : head + 1, low:])).astype(bf16)
            key_sum += dot(grad_scores, query_n[head, low:, :], ((1,), (0,)))
            grad_query_ref[span, low:] += dot(key_t_ref[...], grad_scores, ((1,), (0,)))
        grad_key_ref[...] = key_sum.T
        grad_value_ref[...] = value_sum.T

    for at in range(count):
        pl.when(pl.program_id(0) == at)(functools.partial(keys, at))


def attention_backward(query_t, key_n, key_t, value_n, grad_t, out_t, lse, start):
    width, length = query_t.shape
    heads = width // HD
    block = attention_block(length)
    count = length // block

    def whole(j):
        return 0, 0

    return pl.pallas_call(
        functools.partial(backward_kernel, block, heads, count),
        grid=(count,),
        in_specs=[
            pl.BlockSpec((block, HD), lambda j: (j, 0)),
            pl.BlockSpec((HD, block), lambda j: (0, j)),
            pl.BlockSpec((block, HD), lambda j: (j, 0)),
            pl.BlockSpec((width, length), whole),
            pl.BlockSpec((width, length), whole),
            pl.BlockSpec((width, length), whole),
            pl.BlockSpec((heads, length), whole),
            pl.BlockSpec((1, length), whole),
        ],
        out_specs=[
            pl.BlockSpec((width, length), whole),
            pl.BlockSpec((HD, block), lambda j: (0, j)),
            pl.BlockSpec((HD, block), lambda j: (0, j)),
        ],
        out_shape=[
            jax.ShapeDtypeStruct((width, length), f32),
            jax.ShapeDtypeStruct((HD, length), f32),
            jax.ShapeDtypeStruct((HD, length), f32),
        ],
        scratch_shapes=[
            pltpu.VMEM((heads, length, HD), bf16),
            pltpu.VMEM((heads, length, HD), bf16),
            pltpu.VMEM((heads, length), f32),
        ],
        cost_estimate=pl.CostEstimate(flops=25_000_000_000, transcendentals=0, bytes_accessed=0),
        compiler_params=pltpu.CompilerParams(vmem_limit_bytes=56 * 1024 * 1024),
        name="attention_backward",
    )(key_n, key_t, value_n, query_t, grad_t, out_t, lse, start)


def rotate(source, cosine, sine_part):
    halves = source.reshape(-1, 2, HALF, source.shape[1])
    first, second = halves[:, 0], halves[:, 1]
    turned = jnp.stack(
        [first * cosine - second * sine_part, second * cosine + first * sine_part], axis=1
    )
    return turned.reshape(source.shape)


def body(
    tokens,
    segments,
    cotangent,
    attention_gain,
    query_weight,
    key_weight,
    value_weight,
    projection,
    feedforward_gain,
    gate_weight,
    up_weight,
    down_weight,
):
    seqs, ranks = lax.axis_size("seq"), lax.axis_size("ctx")
    rows = query_weight.shape[0]
    depth = tokens.shape[1]
    units = down_weight.shape[0]
    hidden_units = units * seqs
    local_count = tokens.shape[0]
    length = local_count * ranks
    width = H * HD // ranks

    def row_factor(values):
        return lax.rsqrt(jnp.mean(values * values, axis=-1, keepdims=True) + EPSILON)

    inputs = tokens.astype(f32)
    factor_one = row_factor(inputs)
    own_gains = jnp.concatenate([attention_gain, feedforward_gain]).astype(f32)[None]
    spread, last = double_to(own_gains, seqs)
    tokens_first = gather_first(tokens)

    def split_heads(weight):
        return jnp.repeat(weight.reshape(rows, KV, HD), ranks // KV, axis=1)

    mix = jnp.concatenate(
        [
            query_weight.reshape(rows, ranks, width),
            split_heads(key_weight),
            split_heads(value_weight),
        ],
        axis=2,
    ).transpose(1, 0, 2)
    small = small_rows(spread, segments, mix.shape[2])
    small = jnp.broadcast_to(small[None], (ranks,) + small.shape)
    mix = exchange_ctx(jnp.concatenate([mix, small], axis=1))
    gain_one_row, gain_two_row, seg_row = read_small(mix[:, rows:], spread, segments)
    mix = mix[:, :rows].reshape(ranks * rows, -1)
    proj_wide = gather_seq(lax.ppermute(after(projection, last), BOTH, head_order()))
    mix_wide = gather_seq(after(mix, proj_wide))
    tokens_second = gather_second(lax.optimization_barrier((tokens_first, mix))[0])
    pair = split_units(after(gate_weight, mix), up_weight, units)
    pair = exchange_ctx(pair).reshape(ranks * rows, -1)

    start = jnp.sum((seg_row < seg_row.T).astype(jnp.int32), axis=1)
    positions = jnp.arange(length, dtype=jnp.int32) - start
    freqs = jnp.power(10000.0, -jnp.arange(HALF, dtype=f32) * (2.0 / HD))
    angles = freqs[:, None] * positions.astype(f32)[None, :]
    cosine, sine_part = jnp.cos(angles), jnp.sin(angles)
    start_row = start[None, :]

    def normalize(piece, gain):
        piece = piece.astype(f32)
        return (piece * row_factor(piece) * gain).astype(bf16)

    normed_all = gather_place(tokens_second, True, normalize, (gain_one_row,))
    pair = after(pair, normed_all)
    pair_wide = gather_seq(pair)
    mixed = dot(mix_wide, normed_all, ((0,), (1,)))
    query_t = rotate(mixed[:width], cosine, sine_part).astype(bf16) * bf16(HD**-0.5)
    key_t = rotate(mixed[width : width + HD], cosine, sine_part).astype(bf16)
    value_t = mixed[width + HD :].astype(bf16)
    query_t = after(query_t, pair)
    key_n, value_n = key_t.T, value_t.T
    cotangent_pieces = send_chips(after(cotangent, normed_all))
    out_t, out_low, lse = attention_forward(query_t, key_n, value_t, start_row)
    out_low, cotangent_pieces = lax.optimization_barrier((out_low, cotangent_pieces))
    down_wide = gather_seq(after(down_weight, out_low))
    rows_by = ((1,), (0,))
    hidden = inputs + scatter_pairs(pair_up(out_low, proj_wide, rows_by))

    factor_two = row_factor(hidden)
    normed_two = (hidden * factor_two * gain_two_row).astype(bf16)
    cotangent_pieces, normed_two = lax.optimization_barrier((cotangent_pieces, normed_two))
    normed_two_first = gather_first(normed_two)
    cotangent_all = place_chips(cotangent_pieces, natural=False)
    columns_by = ((1,), (1,))
    normed_two_all = gather_place(gather_second(normed_two_first), natural=False)
    activated, slope, swished = by_rows(
        functools.partial(units_kernel, hidden_units),
        [normed_two_all],
        pair_wide,
        [hidden_units] * 3,
        "hidden_layer",
    )

    grad_down = dot(activated, cotangent_all, ((0,), (0,)), bf16)
    back = functools.partial(units_back_kernel, hidden_units)
    given = [after(cotangent_all, grad_down), slope, swished]
    wide = [2 * hidden_units, depth]
    both = (4, pair_wide)
    back_away, away = by_rows(back, given, down_wide, wide, "hidden_back_away", (1, 2), both)
    given[0] = after(given[0], away)
    given.append(swap(away, 1, ranks))
    back_stay, two_pairs = by_rows(back, given, down_wide, wide, "hidden_back_stay", (0, 2), both)
    two_pairs = blocks_of(two_pairs)
    grad_down = scatter_seq(grad_down).astype(f32)
    two_first, back_stay = scatter_first(two_pairs, back_stay)
    shaped_two = scatter_rest(two_first)[0]
    shaped_two = shaped_two * gain_two_row
    grad_pair = outer(normed_two_all, [back_stay, back_away])
    shaped_two = after(shaped_two, grad_pair)
    grad_pair = scatter_seq(grad_pair)
    mean_two = jnp.mean(shaped_two * hidden, axis=-1, keepdims=True)
    grad_hidden = (
        cotangent.astype(f32)
        + factor_two * shaped_two
        - hidden * (factor_two * factor_two * factor_two * mean_two)
    )

    branch_first, activated = gather_first(grad_hidden.astype(bf16), activated)
    branch_second = gather_second(branch_first)
    away = product([activated], down_wide, rows_by, (1, 2), "out_away")
    given = [after(activated, away), swap(away, 1, ranks)]
    out_pairs = blocks_of(product(given, down_wide, rows_by, (0, 2), "out_stay"))
    branch_second, out_pairs = lax.optimization_barrier((branch_second, out_pairs))
    out_first, _ = scatter_first(out_pairs)
    branch_all = gather_place(branch_second)
    grad_proj = dot(out_low, branch_all, ((0,), (0,)), bf16)
    grad_out_t = after(dot(proj_wide, branch_all, columns_by, bf16), grad_proj)
    grad_out_t, out_first = lax.optimization_barrier((grad_out_t, out_first))
    out_sum, out_last, _ = scatter_rest(out_first)
    grad_out_t = after(grad_out_t, *out_last)
    grad_out_t = after(grad_out_t, grad_pair)
    grad_proj, came = to_owners(grad_proj)
    grad_out_t = after(grad_out_t, *came)
    grad_proj = scatter_seq(grad_proj)
    grad_query_t, grad_key_t, grad_value_t = attention_backward(
        query_t, key_n, key_t, value_n, grad_out_t, out_t, lse, start_row
    )
    grad_mixed = jnp.concatenate(
        [
            rotate(grad_query_t * HD**-0.5, cosine, -sine_part),
            rotate(grad_key_t, cosine, -sine_part),
            grad_value_t,
        ],
        axis=0,
    ).astype(bf16)
    grad_pair = exchange_ctx(grad_pair.reshape(ranks, rows, -1))
    grad_mixed = after(grad_mixed, grad_down, grad_pair, grad_proj)
    block_out = (hidden + out_sum).astype(bf16)
    mixed_n = grad_mixed.T
    core = lax.axis_index("ctx") % 2
    parts = [of_core(mixed_n, 1 - core), of_core(mixed_n, core)]
    away = product(parts[:1], mix_wide, columns_by, None, "mixed_away", LIGHT)
    grad_mix = dot(normed_all, after(grad_mixed, away), ((0,), (1,)), bf16)
    grad_mix = scatter_seq(grad_mix)
    parts = [after(parts[1], away), swap(away, 1, ranks)]
    shaped_one = blocks_of(product(parts, mix_wide, columns_by, None, "mixed_stay", LIGHT))
    grad_gate, grad_up, grad_feedforward = join_units(grad_pair, gate_weight, up_weight, units)
    shaped_first, _ = scatter_first(shaped_one)
    shaped_first = lax.optimization_barrier((shaped_first, grad_gate))[0]
    shaped_one, _, grad_mix = scatter_rest(shaped_first, grad_mix)
    shaped_one = shaped_one * gain_one_row
    mean_one = jnp.mean(shaped_one * inputs, axis=-1, keepdims=True)
    grad_tokens = (
        grad_hidden
        + factor_one * shaped_one
        - inputs * (factor_one * factor_one * factor_one * mean_one)
    )

    def join_heads(part):
        part = part.reshape(KV, ranks // KV, rows, HD).astype(f32).sum(axis=1)
        return part.transpose(1, 0, 2).reshape(rows, -1)

    def row_sum(grad, weight):
        return jnp.sum(grad * weight.astype(f32), axis=1)

    grad_feedforward = grad_feedforward[:, 0] / feedforward_gain.astype(f32)

    grad_mix = exchange_ctx(grad_mix.reshape(ranks, rows, -1))
    grad_query = grad_mix[:, :, :width].transpose(1, 0, 2).reshape(rows, -1).astype(f32)
    grad_key = join_heads(grad_mix[:, :, width : width + HD])
    grad_value = join_heads(grad_mix[:, :, width + HD :])
    grad_attention = (
        row_sum(grad_query, query_weight)
        + row_sum(grad_key, key_weight)
        + row_sum(grad_value, value_weight)
    ) / attention_gain.astype(f32)
    grad_projection = grad_proj.astype(f32)
    return (
        block_out,
        grad_tokens,
        grad_attention,
        grad_query,
        grad_key,
        grad_value,
        grad_projection,
        grad_feedforward,
        grad_gate,
        grad_up,
        grad_down,
    )


def solution(mesh):
    rows, plain = P(BOTH, None), P(BOTH)
    return jax.shard_map(
        body,
        mesh=mesh,
        in_specs=(rows, P("seq", "ctx"), rows, plain, rows, rows, rows, rows, plain, rows, rows, rows),
        out_specs=(rows, rows, plain, rows, rows, rows, rows, plain, rows, rows, rows),
        check_vma=False,
    )
```

```python
import functools

import jax
import jax.numpy as jnp
from jax import lax
from jax.experimental import pallas as pl
from jax.experimental.pallas import tpu as pltpu
from jax.sharding import PartitionSpec as P

H = 32
KV = 4
HD = 64
HALF = HD // 2

EPSILON = 1e-05
MASKED = -1e30
BOTH = ("seq", "ctx")
f32 = jnp.float32
bf16 = jnp.bfloat16
LIGHT = pl.CostEstimate(flops=0, transcendentals=0, bytes_accessed=0)


def dot(left, right, contract, out=f32):
    return lax.dot_general(left, right, (contract, ((), ())), preferred_element_type=f32).astype(out)


def after(value, *others):
    return lax.optimization_barrier((value, *others))[0]


def swap(value, step, count):
    return lax.ppermute(value, "ctx", [(i, i ^ step) for i in range(count)])


def blank(shape, dtype):
    return pl.pallas_call(
        lambda out_ref: None,
        out_shape=jax.ShapeDtypeStruct(shape, dtype),
        out_specs=pl.BlockSpec(memory_space=pl.ANY),
        name="blank",
    )()


def chip_bits():
    me = lax.axis_index("ctx")
    count = lax.axis_size("ctx")
    bits = [1 << at for at in range(1, count.bit_length() - 1)]
    return [(step, (me // step) % 2) for step in bits]


def gather_first(value, beside=None):
    count = lax.axis_size("ctx")
    bits = chip_bits()
    half = value.shape[0] // 2
    steps = (bits[0][0], bits[-1][0])
    parts = [value[:half], value[half:]]
    if beside is not None:
        parts, beside = lax.optimization_barrier((parts, beside))
    first = [(part, swap(part, step, count)) for part, step in zip(parts, steps)]
    return first if beside is None else (first, beside)


def gather_second(first):
    count = lax.axis_size("ctx")
    bits = chip_bits()
    parts = []
    for which, (current, arrived) in enumerate(first):
        half, depth = current.shape
        order = list(range(len(bits)))
        if which:
            order.reverse()
        current = current.reshape((1,) * len(bits) + (half, depth))
        arrived = arrived.reshape(current.shape)
        for at in order:
            step, bit = bits[at]
            axis = len(bits) - 1 - at
            if at != order[0]:
                arrived = swap(current, step, count)
            if at != order[-1]:
                current = jnp.where(
                    bit == 0,
                    jnp.concatenate([current, arrived], axis),
                    jnp.concatenate([arrived, current], axis),
                )
        parts.append((current, arrived))
    return parts


def place_kernel(bits, steps, natural, change, *refs):
    parts = 4 * 2
    given, gains = refs[:parts], refs[parts:-4]
    whole, held, ready, done = refs[-4:]
    me = lax.axis_index("ctx")
    core = lax.rem(me, 2)
    arrivals = [pltpu.make_async_copy(ref, held.at[i], ready.at[i]) for i, ref in enumerate(given)]
    copies = []
    for arrival in arrivals:
        arrival.start()
    for number, arrival in enumerate(arrivals):
        which, late, there = number // 4, number // 2 % 2, number % 2
        at = 0 if which else bits - 1
        axis = bits - 1 - at
        index = lax.rem(me // steps[at], 2)
        index = 1 - index if late else index
        owner = 1 - core if there else core
        spot = [slice(None)] * bits
        spot[axis] = index
        arrival.wait()
        if change is not None:
            held[number] = change(held[number], *[ref[...] for ref in gains])
        place = (*spot, owner, which) if natural else (there, *spot, which)
        copy = pltpu.make_async_copy(held.at[number], whole.at[place], done.at[number])
        copy.start()
        copies.append(copy)
    for copy in copies:
        copy.wait()


def gather_place(parts, natural=True, change=None, gains=()):
    count = lax.axis_size("ctx")
    steps = tuple(step for step, _ in chip_bits())
    half, depth = parts[0][0].shape[-2:]
    pieces = []
    for pair in parts:
        for part in pair:
            pieces += [part, swap(part, 1, count)]
    pieces = [piece.reshape((2,) * (len(steps) - 1) + (half, depth)) for piece in pieces]
    anywhere = pl.BlockSpec(memory_space=pl.ANY)
    dtype = pieces[0].dtype
    whole = pl.pallas_call(
        functools.partial(place_kernel, len(steps), steps, natural, change),
        in_specs=[anywhere] * len(pieces) + [pl.BlockSpec(memory_space=pltpu.VMEM)] * len(gains),
        out_specs=anywhere,
        out_shape=jax.ShapeDtypeStruct((2,) * len(steps) + (2, 2, half, depth), dtype),
        scratch_shapes=[
            pltpu.VMEM((len(pieces),) + pieces[0].shape, dtype),
            pltpu.SemaphoreType.DMA((len(pieces),)),
            pltpu.SemaphoreType.DMA((len(pieces),)),
        ],
        compiler_params=pltpu.CompilerParams(vmem_limit_bytes=48 * 1024 * 1024),
        cost_estimate=LIGHT,
        name="place",
    )(*pieces, *gains)
    return whole.reshape(2 * count * half, depth)


def send_chips(value):
    count = lax.axis_size("ctx")
    return {step: swap(value, step, count) if step else value for step in range(0, count, 2)}


def place_chips(pieces, natural=True):
    count = lax.axis_size("ctx")
    me = lax.axis_index("ctx")
    whole = blank((count,) + pieces[0].shape, pieces[0].dtype)
    for step, piece in pieces.items():
        for there in range(2):
            spot = me ^ step ^ there if natural else there * (count // 2) + (me ^ step) // 2
            piece = swap(piece, 1, count) if there else piece
            whole = lax.dynamic_update_index_in_dim(whole, piece, spot, 0)
    return whole.reshape((-1,) + pieces[0].shape[1:])


def double(value, step):
    seqs = lax.axis_size("seq")
    bit = (lax.axis_index("seq") // step) % 2
    other = lax.ppermute(value, "seq", [(i, i ^ step) for i in range(seqs)])
    whole = jnp.where(bit == 0, jnp.concatenate([value, other]), jnp.concatenate([other, value]))
    return whole, other


def double_to(value, end):
    step, other = 1, value
    while step < end:
        value, other = double(value, step)
        step *= 2
    return value, other


def head_order():
    seqs, ranks = lax.axis_size("seq"), lax.axis_size("ctx")
    return [(i, (i % seqs) * ranks + i // seqs) for i in range(seqs * ranks)]


def to_owners(value):
    seqs, ranks = lax.axis_size("seq"), lax.axis_size("ctx")
    me = lax.axis_index("ctx")
    share = ranks // seqs
    blocks = value.reshape(seqs, -1, value.shape[1])
    whole = blank(blocks.shape, value.dtype)
    came = []
    for turn in range(seqs):
        piece = lax.dynamic_index_in_dim(blocks, (me // share + seqs - turn) % seqs, 0, False)
        pairs = [(r, r % share * seqs + (r // share - turn) % seqs) for r in range(ranks)]
        came.append(lax.ppermute(piece, "ctx", pairs))
        spot = (me % seqs + turn) % seqs
        whole = lax.dynamic_update_index_in_dim(whole, came[-1], spot, 0)
    return whole.reshape(value.shape), came


def of_core(value, core):
    count = lax.axis_size("ctx")
    blocks = value.reshape(count // 2, 2, value.shape[0] // count, value.shape[1])
    return lax.dynamic_index_in_dim(blocks, core, 1, keepdims=False).reshape(-1, value.shape[1])


def blocks_of(pairs):
    return pairs.reshape(lax.axis_size("ctx") // 2, -1, pairs.shape[1])


def pair_up(left, right, contract):
    core = lax.axis_index("ctx") % 2
    away = dot(of_core(left, 1 - core), right, contract, bf16)
    arrived = swap(away, 1, lax.axis_size("ctx"))
    stay = after(of_core(left, core), away)
    return blocks_of((dot(stay, right, contract) + arrived.astype(f32)).astype(bf16))


def scatter_parts(current, at):
    bit = chip_bits()[at][1]
    axis = current.ndim - 3 - at
    stay = lax.dynamic_slice_in_dim(current, bit, 1, axis).astype(f32)
    return stay, lax.dynamic_slice_in_dim(current, 1 - bit, 1, axis).astype(bf16)


def scatter_first(pairs, beside=()):
    count = lax.axis_size("ctx")
    bits = chip_bits()
    half, depth = pairs.shape[1] // 2, pairs.shape[2]
    pairs = pairs.reshape((2,) * len(bits) + (2, half, depth))
    low = scatter_parts(pairs[..., 0, :, :], 0)
    high = scatter_parts(pairs[..., 1, :, :], len(bits) - 1)
    aways, beside = lax.optimization_barrier(((low[1], high[1]), beside))
    first = [
        (stay, swap(away, bits[at][0], count))
        for (stay, _), away, at in ((low, aways[0], 0), (high, aways[1], len(bits) - 1))
    ]
    return first, beside


def scatter_rest(first):
    count = lax.axis_size("ctx")
    bits = chip_bits()
    last = []
    sums = []
    for which, (stay, arrived) in enumerate(first):
        for at in range(1, len(bits)):
            at = len(bits) - 1 - at if which else at
            stay, away = scatter_parts(stay + arrived.astype(f32), at)
            arrived = swap(away, bits[at][0], count)
        last.append(arrived)
        sums.append(stay + arrived.astype(f32))
    return jnp.concatenate([part.reshape(part.shape[-2:]) for part in sums]), last


def scatter_pairs(pairs):
    return scatter_rest(scatter_first(pairs)[0])[0]


def gather_seq(value):
    return lax.all_gather(value, "seq", axis=0, tiled=True)


def scatter_seq(value):
    return lax.psum_scatter(value, "seq", scatter_dimension=0, tiled=True)


def exchange_ctx(value):
    return lax.all_to_all(value, "ctx", 0, 0)


def small_rows(spread, segments, width):
    line = jnp.concatenate([spread.reshape(-1), segments.reshape(-1).astype(f32)]).astype(bf16)
    count = -(-line.size // (16 * width)) * 16
    return jnp.pad(line, (0, count * width - line.size)).reshape(count, width)


def read_small(table, spread, segments):
    ranks, seqs = table.shape[0], spread.shape[0]
    table = table.reshape(ranks, -1)
    width, count = spread.size, segments.size
    gains = table[:, :width].reshape(ranks, seqs, 2, -1).transpose(2, 1, 0, 3).reshape(2, -1)
    gains = gains.astype(f32)
    return gains[:1], gains[1:], table[:, width : width + count].astype(f32).reshape(1, -1)


def unit_pieces(seqs, ranks, units):
    wide = seqs * units
    main = wide // 128 * 128
    for rank in range(ranks):
        for which in range(2):
            for seq in range(seqs):
                first, at, end = (seq * ranks + rank) * units, seq * units, (seq + 1) * units
                if at < main:
                    yield rank, which, first, which * main + at, min(end, main) - at
                if end > main:
                    cut = max(at, main)
                    to = 2 * main + which * (wide - main) + cut - main
                    yield rank, which, first + cut - at, to, end - cut


def split_kernel(pieces, gate_ref, up_ref, out_ref):
    refs = (gate_ref, up_ref)
    for rank, which, first, to, size in pieces:
        out_ref[rank, :, to : to + size] = refs[which][:, first : first + size]


def split_units(gate, up, units):
    seqs, ranks = lax.axis_size("seq"), lax.axis_size("ctx")
    return pl.pallas_call(
        functools.partial(split_kernel, tuple(unit_pieces(seqs, ranks, units))),
        out_shape=jax.ShapeDtypeStruct((ranks, gate.shape[0], 2 * seqs * units), gate.dtype),
        compiler_params=pltpu.CompilerParams(vmem_limit_bytes=48 * 1024 * 1024),
        name="split_units",
    )(gate, up)


def join_kernel(pieces, grad_ref, gate_ref, up_ref, grad_gate_ref, grad_up_ref, sum_ref):
    refs = (grad_gate_ref, grad_up_ref)
    for rank, which, first, to, size in pieces:
        refs[which][:, first : first + size] = grad_ref[rank, :, to : to + size].astype(f32)
    terms = grad_gate_ref[...] * gate_ref[...].astype(f32)
    terms = terms + grad_up_ref[...] * up_ref[...].astype(f32)
    sum_ref[...] = jnp.sum(terms, axis=1, keepdims=True)


def join_units(grad, gate, up, units):
    seqs, ranks = lax.axis_size("seq"), lax.axis_size("ctx")
    whole = jax.ShapeDtypeStruct(gate.shape, f32)
    return pl.pallas_call(
        functools.partial(join_kernel, tuple(unit_pieces(seqs, ranks, units))),
        out_shape=[whole, whole, jax.ShapeDtypeStruct((gate.shape[0], 1), f32)],
        compiler_params=pltpu.CompilerParams(vmem_limit_bytes=48 * 1024 * 1024),
        name="join_units",
    )(grad, gate, up)


def spans_of(hidden):
    main = hidden // 128 * 128
    return [(0, main)] + ([(main, hidden - main)] if main < hidden else [])


def units_kernel(hidden, row_ref, weight_ref, out_ref, slope_ref, swished_ref):
    both = dot(row_ref[...], weight_ref[...], ((1,), (0,)))
    for first, size in spans_of(hidden):
        span = slice(first, first + size)
        gate = both[:, 2 * first : 2 * first + size]
        upward = both[:, 2 * first + size : 2 * first + 2 * size]
        sigmoid_gate = jax.nn.sigmoid(gate)
        swished = gate * sigmoid_gate
        out_ref[:, span] = (swished * upward).astype(bf16)
        slope_ref[:, span] = (upward * sigmoid_gate * (1.0 + gate * (1.0 - sigmoid_gate))).astype(bf16)
        swished_ref[:, span] = swished.astype(bf16)


def units_back_kernel(hidden, grad_ref, down_ref, slope_ref, swished_ref, weight_ref, *refs):
    *given, out_ref, product_ref = refs
    grads = dot(grad_ref[...], down_ref[...], ((1,), (1,)))
    for first, size in spans_of(hidden):
        span = slice(first, first + size)
        grad = grads[:, span]
        out_ref[:, 2 * first : 2 * first + size] = (grad * slope_ref[:, span].astype(f32)).astype(bf16)
        out_ref[:, 2 * first + size : 2 * first + 2 * size] = (
            grad * swished_ref[:, span].astype(f32)
        ).astype(bf16)
    product = dot(out_ref[...], weight_ref[...], ((1,), (1,)))
    for ref in given:
        product = product + ref[...].astype(f32)
    product_ref[...] = product.astype(bf16)


def product_kernel(contract, row_ref, weight_ref, *refs):
    out = dot(row_ref[...], weight_ref[...], contract)
    for ref in refs[:-1]:
        out = out + ref[...].astype(f32)
    refs[-1][...] = out.astype(bf16)


def by_rows(kernel, rows, weight, widths, name, part=None, also=None, cost=LIGHT):
    number, parts = part or (0, 1)
    count = rows[0].shape[0] // parts
    block = 256 if count % 256 == 0 else count

    def spec(array):
        first = number * (count // block) if array.shape[0] != count else 0
        return pl.BlockSpec((block, array.shape[1]), lambda i: (i + first, 0))

    arrays = list(rows)
    specs = [spec(array) for array in rows]
    for place, whole in ((1, weight), also or (0, None)):
        if whole is not None:
            arrays.insert(place, whole)
            specs.insert(place, pl.BlockSpec(whole.shape, lambda i: (0, 0)))
    return pl.pallas_call(
        kernel,
        grid=(count // block,),
        in_specs=specs,
        out_specs=[pl.BlockSpec((block, width), lambda i: (i, 0)) for width in widths],
        out_shape=[jax.ShapeDtypeStruct((count, width), bf16) for width in widths],
        compiler_params=pltpu.CompilerParams(vmem_limit_bytes=56 * 1024 * 1024),
        cost_estimate=cost,
        name=name,
    )(*arrays)


HIDDEN_COST = pl.CostEstimate(flops=7_000_000_000, transcendentals=0, bytes_accessed=0)


def product(rows, weight, contract, part, name, cost=HIDDEN_COST):
    kernel = functools.partial(product_kernel, contract)
    width = weight.shape[1 - contract[1][0]]
    return by_rows(kernel, rows, weight, [width], name, part, None, cost)[0]


def outer_kernel(row_ref, *refs):
    *others, out_ref = refs
    first, total = 0, 0.0
    for ref in others:
        end = first + ref.shape[0]
        total = total + dot(row_ref[first:end, :], ref[...], ((0,), (0,)))
        first = end
    out_ref[...] = total.astype(bf16)


def outer(row, others):
    count, depth = row.shape
    width = others[0].shape[1]
    block = 512 if depth % 512 == 0 else depth
    return pl.pallas_call(
        outer_kernel,
        grid=(depth // block,),
        in_specs=[pl.BlockSpec((count, block), lambda i: (0, i))]
        + [pl.BlockSpec(other.shape, lambda i: (0, 0)) for other in others],
        out_specs=pl.BlockSpec((block, width), lambda i: (i, 0)),
        out_shape=jax.ShapeDtypeStruct((depth, width), bf16),
        compiler_params=pltpu.CompilerParams(vmem_limit_bytes=56 * 1024 * 1024),
        cost_estimate=LIGHT,
        name="outer",
    )(row, *others)


def attention_block(length):
    return 512 if length % 512 == 0 else length


def forward_kernel(
    block, heads, count, key_ref, value_ref, query_ref, start_ref, out_ref, out_n_ref, lse_ref
):
    def queries(at):
        end = (at + 1) * block
        rows = lax.broadcasted_iota(jnp.int32, (end, block), 0)
        columns = lax.broadcasted_iota(jnp.int32, (end, block), 1) + at * block
        allowed = (rows >= start_ref[...]) & (rows <= columns)
        for head in range(heads):
            span = slice(head * HD, (head + 1) * HD)
            scores = dot(key_ref[:end, :], query_ref[span, :], ((1,), (0,)))
            scores = jnp.where(allowed, scores, MASKED)
            top = jnp.max(scores, axis=0, keepdims=True)
            weights = jnp.exp(scores - top)
            mass = jnp.sum(weights, axis=0, keepdims=True)
            out = dot(value_ref[:, :end], weights.astype(bf16), ((1,), (0,))) / mass
            out_ref[span, :] = out
            out_n_ref[:, span] = out.T.astype(bf16)
            lse_ref[head : head + 1, :] = top + jnp.log(mass)

    for at in range(count):
        pl.when(pl.program_id(0) == at)(functools.partial(queries, at))


def attention_forward(query_t, key_n, value_t, start):
    width, length = query_t.shape
    heads = width // HD
    block = attention_block(length)
    return pl.pallas_call(
        functools.partial(forward_kernel, block, heads, length // block),
        grid=(length // block,),
        in_specs=[
            pl.BlockSpec((length, HD), lambda i: (0, 0)),
            pl.BlockSpec((HD, length), lambda i: (0, 0)),
            pl.BlockSpec((width, block), lambda i: (0, i)),
            pl.BlockSpec((1, block), lambda i: (0, i)),
        ],
        out_specs=[
            pl.BlockSpec((width, block), lambda i: (0, i)),
            pl.BlockSpec((block, width), lambda i: (i, 0)),
            pl.BlockSpec((heads, block), lambda i: (0, i)),
        ],
        out_shape=[
            jax.ShapeDtypeStruct((width, length), f32),
            jax.ShapeDtypeStruct((length, width), bf16),
            jax.ShapeDtypeStruct((heads, length), f32),
        ],
        compiler_params=pltpu.CompilerParams(vmem_limit_bytes=56 * 1024 * 1024),
        cost_estimate=LIGHT,
        name="attention_forward",
    )(key_n, value_t, query_t, start)


def backward_kernel(
    block,
    heads,
    count,
    key_ref,
    key_t_ref,
    value_ref,
    query_ref,
    grad_ref,
    out_ref,
    lse_ref,
    start_ref,
    grad_query_ref,
    grad_key_ref,
    grad_value_ref,
    query_n,
    grad_n,
    delta,
):
    spans = [slice(head * HD, (head + 1) * HD) for head in range(heads)]

    @pl.when(pl.program_id(0) == 0)
    def _():
        grad_query_ref[...] = jnp.zeros_like(grad_query_ref)
        for head, span in enumerate(spans):
            grads = grad_ref[span, :].astype(f32)
            query_n[head] = query_ref[span, :].astype(f32).T.astype(bf16)
            grad_n[head] = grads.T.astype(bf16)
            delta[head : head + 1, :] = jnp.sum(grads * out_ref[span, :], axis=0, keepdims=True)

    def keys(at):
        low = at * block
        shape = (block, (count - at) * block)
        rows = lax.broadcasted_iota(jnp.int32, shape, 0) + low
        columns = lax.broadcasted_iota(jnp.int32, shape, 1) + low
        allowed = (rows >= start_ref[:, low:]) & (rows <= columns)
        key_sum = jnp.zeros((block, HD), f32)
        value_sum = jnp.zeros((block, HD), f32)
        for head, span in enumerate(spans):
            scores = dot(key_ref[...], query_ref[span, low:], ((1,), (0,)))
            scores = jnp.where(allowed, scores, MASKED)
            probs = jnp.exp(scores - lse_ref[head : head + 1, low:])
            value_sum += dot(probs.astype(bf16), grad_n[head, low:, :], ((1,), (0,)))
            grad_probs = dot(value_ref[...], grad_ref[span, low:], ((1,), (0,)))
            grad_scores = (probs * (grad_probs - delta[head : head + 1, low:])).astype(bf16)
            key_sum += dot(grad_scores, query_n[head, low:, :], ((1,), (0,)))
            grad_query_ref[span, low:] += dot(key_t_ref[...], grad_scores, ((1,), (0,)))
        grad_key_ref[...] = key_sum.T
        grad_value_ref[...] = value_sum.T

    for at in range(count):
        pl.when(pl.program_id(0) == at)(functools.partial(keys, at))


def attention_backward(query_t, key_n, key_t, value_n, grad_t, out_t, lse, start):
    width, length = query_t.shape
    heads = width // HD
    block = attention_block(length)
    count = length // block

    def whole(j):
        return 0, 0

    return pl.pallas_call(
        functools.partial(backward_kernel, block, heads, count),
        grid=(count,),
        in_specs=[
            pl.BlockSpec((block, HD), lambda j: (j, 0)),
            pl.BlockSpec((HD, block), lambda j: (0, j)),
            pl.BlockSpec((block, HD), lambda j: (j, 0)),
            pl.BlockSpec((width, length), whole),
            pl.BlockSpec((width, length), whole),
            pl.BlockSpec((width, length), whole),
            pl.BlockSpec((heads, length), whole),
            pl.BlockSpec((1, length), whole),
        ],
        out_specs=[
            pl.BlockSpec((width, length), whole),
            pl.BlockSpec((HD, block), lambda j: (0, j)),
            pl.BlockSpec((HD, block), lambda j: (0, j)),
        ],
        out_shape=[
            jax.ShapeDtypeStruct((width, length), f32),
            jax.ShapeDtypeStruct((HD, length), f32),
            jax.ShapeDtypeStruct((HD, length), f32),
        ],
        scratch_shapes=[
            pltpu.VMEM((heads, length, HD), bf16),
            pltpu.VMEM((heads, length, HD), bf16),
            pltpu.VMEM((heads, length), f32),
        ],
        cost_estimate=pl.CostEstimate(flops=25_000_000_000, transcendentals=0, bytes_accessed=0),
        compiler_params=pltpu.CompilerParams(vmem_limit_bytes=56 * 1024 * 1024),
        name="attention_backward",
    )(key_n, key_t, value_n, query_t, grad_t, out_t, lse, start)


def rotate(source, cosine, sine_part):
    halves = source.reshape(-1, 2, HALF, source.shape[1])
    first, second = halves[:, 0], halves[:, 1]
    turned = jnp.stack(
        [first * cosine - second * sine_part, second * cosine + first * sine_part], axis=1
    )
    return turned.reshape(source.shape)


def body(
    tokens,
    segments,
    cotangent,
    attention_gain,
    query_weight,
    key_weight,
    value_weight,
    projection,
    feedforward_gain,
    gate_weight,
    up_weight,
    down_weight,
):
    seqs, ranks = lax.axis_size("seq"), lax.axis_size("ctx")
    rows = query_weight.shape[0]
    depth = tokens.shape[1]
    units = down_weight.shape[0]
    hidden_units = units * seqs
    local_count = tokens.shape[0]
    length = local_count * ranks
    width = H * HD // ranks

    def row_factor(values):
        return lax.rsqrt(jnp.mean(values * values, axis=-1, keepdims=True) + EPSILON)

    inputs = tokens.astype(f32)
    factor_one = row_factor(inputs)
    own_gains = jnp.concatenate([attention_gain, feedforward_gain]).astype(f32)[None]
    spread, _ = double_to(own_gains, seqs)
    tokens_first = gather_first(tokens)

    def split_heads(weight):
        return jnp.repeat(weight.reshape(rows, KV, HD), ranks // KV, axis=1)

    mix = jnp.concatenate(
        [
            query_weight.reshape(rows, ranks, width),
            split_heads(key_weight),
            split_heads(value_weight),
        ],
        axis=2,
    ).transpose(1, 0, 2)
    small = small_rows(spread, segments, mix.shape[2])
    small = jnp.broadcast_to(small[None], (ranks,) + small.shape)
    mix = exchange_ctx(jnp.concatenate([mix, small], axis=1))
    gain_one_row, gain_two_row, seg_row = read_small(mix[:, rows:], spread, segments)
    mix = mix[:, :rows].reshape(ranks * rows, -1)
    proj_wide = gather_seq(lax.ppermute(projection, BOTH, head_order()))
    mix_wide = gather_seq(after(mix, proj_wide))
    tokens_second = gather_second(lax.optimization_barrier((tokens_first, mix))[0])
    pair = split_units(after(gate_weight, mix), up_weight, units)
    pair = exchange_ctx(pair).reshape(ranks * rows, -1)

    start = jnp.sum((seg_row < seg_row.T).astype(jnp.int32), axis=1)
    positions = jnp.arange(length, dtype=jnp.int32) - start
    freqs = jnp.power(10000.0, -jnp.arange(HALF, dtype=f32) * (2.0 / HD))
    angles = freqs[:, None] * positions.astype(f32)[None, :]
    cosine, sine_part = jnp.cos(angles), jnp.sin(angles)
    start_row = start[None, :]

    def normalize(piece, gain):
        piece = piece.astype(f32)
        return (piece * row_factor(piece) * gain).astype(bf16)

    normed_all = gather_place(tokens_second, True, normalize, (gain_one_row,))
    pair = after(pair, normed_all)
    pair_wide = gather_seq(pair)
    mixed = dot(mix_wide, normed_all, ((0,), (1,)))
    query_t = rotate(mixed[:width], cosine, sine_part).astype(bf16) * bf16(HD**-0.5)
    key_t = rotate(mixed[width : width + HD], cosine, sine_part).astype(bf16)
    value_t = mixed[width + HD :].astype(bf16)
    query_t = after(query_t, pair)
    key_n, value_n = key_t.T, value_t.T
    cotangent_pieces = send_chips(after(cotangent, normed_all))
    out_t, out_low, lse = attention_forward(query_t, key_n, value_t, start_row)
    out_low, cotangent_pieces = lax.optimization_barrier((out_low, cotangent_pieces))
    down_wide = gather_seq(after(down_weight, out_low))
    rows_by = ((1,), (0,))
    hidden = inputs + scatter_pairs(pair_up(out_low, proj_wide, rows_by))

    factor_two = row_factor(hidden)
    normed_two = (hidden * factor_two * gain_two_row).astype(bf16)
    cotangent_pieces, normed_two = lax.optimization_barrier((cotangent_pieces, normed_two))
    normed_two_first = gather_first(normed_two)
    cotangent_all = place_chips(cotangent_pieces, natural=False)
    columns_by = ((1,), (1,))
    normed_two_all = gather_place(gather_second(normed_two_first), natural=False)
    activated, slope, swished = by_rows(
        functools.partial(units_kernel, hidden_units),
        [normed_two_all],
        pair_wide,
        [hidden_units] * 3,
        "hidden_layer",
    )

    grad_down = dot(activated, cotangent_all, ((0,), (0,)), bf16)
    back = functools.partial(units_back_kernel, hidden_units)
    given = [after(cotangent_all, grad_down), slope, swished]
    wide = [2 * hidden_units, depth]
    both = (4, pair_wide)
    back_away, away = by_rows(back, given, down_wide, wide, "hidden_back_away", (1, 2), both)
    given[0] = after(given[0], away)
    given.append(swap(away, 1, ranks))
    back_stay, two_pairs = by_rows(back, given, down_wide, wide, "hidden_back_stay", (0, 2), both)
    two_pairs = blocks_of(two_pairs)
    grad_down = scatter_seq(grad_down).astype(f32)
    two_first, back_stay = scatter_first(two_pairs, back_stay)
    shaped_two, _ = scatter_rest(two_first)
    shaped_two = shaped_two * gain_two_row
    grad_pair = outer(normed_two_all, [back_stay, back_away])
    shaped_two = after(shaped_two, grad_pair)
    grad_pair = scatter_seq(grad_pair)
    mean_two = jnp.mean(shaped_two * hidden, axis=-1, keepdims=True)
    grad_hidden = (
        cotangent.astype(f32)
        + factor_two * shaped_two
        - hidden * (factor_two * factor_two * factor_two * mean_two)
    )

    branch_first, activated = gather_first(grad_hidden.astype(bf16), activated)
    branch_second = gather_second(branch_first)
    away = product([activated], down_wide, rows_by, (1, 2), "out_away")
    given = [after(activated, away), swap(away, 1, ranks)]
    out_pairs = blocks_of(product(given, down_wide, rows_by, (0, 2), "out_stay"))
    branch_second, out_pairs = lax.optimization_barrier((branch_second, out_pairs))
    out_first, _ = scatter_first(out_pairs)
    branch_all = gather_place(branch_second)
    grad_proj = dot(out_low, branch_all, ((0,), (0,)), bf16)
    grad_out_t = after(dot(proj_wide, branch_all, columns_by, bf16), grad_proj)
    grad_out_t, out_first = lax.optimization_barrier((grad_out_t, out_first))
    out_sum, out_last = scatter_rest(out_first)
    grad_out_t = after(grad_out_t, *out_last)
    grad_out_t = after(grad_out_t, grad_pair)
    grad_proj, came = to_owners(grad_proj)
    grad_out_t = after(grad_out_t, *came)
    grad_proj = scatter_seq(grad_proj)
    grad_query_t, grad_key_t, grad_value_t = attention_backward(
        query_t, key_n, key_t, value_n, grad_out_t, out_t, lse, start_row
    )
    grad_mixed = jnp.concatenate(
        [
            rotate(grad_query_t * HD**-0.5, cosine, -sine_part),
            rotate(grad_key_t, cosine, -sine_part),
            grad_value_t,
        ],
        axis=0,
    ).astype(bf16)
    grad_pair = exchange_ctx(grad_pair.reshape(ranks, rows, -1))
    grad_mixed = after(grad_mixed, grad_down, grad_pair, grad_proj)
    block_out = (hidden + out_sum).astype(bf16)
    mixed_n = grad_mixed.T
    core = lax.axis_index("ctx") % 2
    parts = [of_core(mixed_n, 1 - core), of_core(mixed_n, core)]
    away = product(parts[:1], mix_wide, columns_by, None, "mixed_away", LIGHT)
    grad_mix = dot(normed_all, after(grad_mixed, away), ((0,), (1,)), bf16)
    grad_mix = scatter_seq(grad_mix)
    parts = [after(parts[1], away), swap(away, 1, ranks)]
    shaped_one = blocks_of(product(parts, mix_wide, columns_by, None, "mixed_stay", LIGHT))
    grad_gate, grad_up, grad_feedforward = join_units(grad_pair, gate_weight, up_weight, units)
    shaped_first, _ = scatter_first(shaped_one)
    shaped_first, grad_mix = lax.optimization_barrier(
        (shaped_first, grad_mix, grad_gate)
    )[:2]
    shaped_one, arrived = scatter_rest(shaped_first)
    shaped_one = shaped_one * gain_one_row
    mean_one = jnp.mean(shaped_one * inputs, axis=-1, keepdims=True)
    grad_tokens = (
        grad_hidden
        + factor_one * shaped_one
        - inputs * (factor_one * factor_one * factor_one * mean_one)
    )

    def join_heads(part):
        part = part.reshape(KV, ranks // KV, rows, HD).astype(f32).sum(axis=1)
        return part.transpose(1, 0, 2).reshape(rows, -1)

    def row_sum(grad, weight):
        return jnp.sum(grad * weight.astype(f32), axis=1)

    grad_feedforward = grad_feedforward[:, 0] / feedforward_gain.astype(f32)

    grad_mix = exchange_ctx(grad_mix.reshape(ranks, rows, -1))
    grad_query = grad_mix[:, :, :width].transpose(1, 0, 2).reshape(rows, -1).astype(f32)
    grad_key = join_heads(grad_mix[:, :, width : width + HD])
    grad_value = join_heads(grad_mix[:, :, width + HD :])
    grad_attention = (
        row_sum(grad_query, query_weight)
        + row_sum(grad_key, key_weight)
        + row_sum(grad_value, value_weight)
    ) / attention_gain.astype(f32)
    grad_projection = grad_proj.astype(f32)
    return (
        block_out,
        grad_tokens,
        grad_attention,
        grad_query,
        grad_key,
        grad_value,
        grad_projection,
        grad_feedforward,
        grad_gate,
        grad_up,
        grad_down,
    )


def solution(mesh):
    rows, plain = P(BOTH, None), P(BOTH)
    return jax.shard_map(
        body,
        mesh=mesh,
        in_specs=(rows, P("seq", "ctx"), rows, plain, rows, rows, rows, rows, plain, rows, rows, rows),
        out_specs=(rows, rows, plain, rows, rows, rows, rows, plain, rows, rows, rows),
        check_vma=False,
    )
```
